512 devices in a mesh: ctx: 8 (over x, core), exp: 64 (over z, y).
Axes of the slice: x: 4, y: 4, z: 16, core: 2. Of those that a mesh axis runs over, the one named last changes fastest.
Arguments:
- queries: bfloat16 [64, 2, 576, 128], P('exp'), may hold values from -110 to 110
- latent_key_cache: bfloat16 [64, 576, 4096], P('exp', None, 'ctx'), may hold values from -6 to 6
- cache_lengths: int32 [64], P('exp'), may hold values from 1024 to 4096, as said below
- token_rows: bfloat16 [1024, 7168], P('exp'), may hold values from -6 to 6
- expert_ids: int32 [1024, 8], P('exp'), may hold values from 0 to 63, all different within a row; in each aligned block of 16 rows (0 to 15, 16 to 31, ...) at most 4 rows name the same one
- gate_scores: float32 [1024, 8], P('exp'), may hold values from 0.1 to 1
- up_maps: bfloat16 [64, 7168, 1024], P('exp', None, 'ctx'), may hold values from -0.0625 to 0.0625
- down_maps: bfloat16 [64, 1024, 7168], P('exp', 'ctx'), may hold values from -0.1875 to 0.1875
Outputs:
- attended: bfloat16 [64, 2, 128, 512], P('exp', None, 'ctx')
- combined: bfloat16 [1024, 7168], P('exp', 'ctx')
The draws below stay inside these ranges and needn't reach their ends.
Inputs may be any that keep to these rules, and one draw needn't show every extreme that they name: `cache_lengths`: counts the 2 new positions; the first sequence's cache is full. `expert_ids`: each row names 8 different experts; among the rows of one index of exp no expert is named more than 4 times, and on some index some expert exactly 4 times.
All inputs are finite; a program needn't handle non-finite values.
Results may differ from the reference program's by a relative error of at most 0.0064.
Values may be sent and summed in bfloat16 or wider, within the bound.
A program may use at most 64 MiB of HBM per device.

```python
import math
import jax
import jax.numpy as jnp
import numpy as np
from jax import lax

D = 7168
HEADS = 128
LATENT_RANK = 512
TOP = 8
FF_HID = 1024
STEPS = 2
ROWS_DEV = 16
EXPERTS = 64
SEQS = 64
NCTX = 4096
LAT_ALL = 576
TOKENS = 1024
CAPD = 4
N_CTX = 8
N_EXP = 64


def cache_field(key):
    return jnp.clip(jax.random.normal(key, (SEQS, LAT_ALL, NCTX), jnp.float32), -6.0, 6.0)


def draw_latent_key_cache(key, part):
    return cache_field(key).astype(jnp.bfloat16)


def draw_queries(key, part):
    key = jax.random.fold_in(key, 7)
    base = jnp.clip(jax.random.normal(key, (SEQS, STEPS, LAT_ALL, HEADS), jnp.float32) * 0.6, -3.6, 3.6)
    return base.astype(jnp.bfloat16)


def draw_cache_lengths(key, part):
    key = jax.random.fold_in(key, 11)
    lengths = jax.random.randint(key, (SEQS,), NCTX // 4, NCTX + 1).astype(jnp.int32)
    return lengths.at[0].set(NCTX)


def levels(own_key, shape, pieces, low, top_value):
    gain = 1.0
    for position, parts in pieces:
        draws = jax.random.uniform(jax.random.fold_in(jax.random.fold_in(own_key, 6), position), (parts,), jnp.float32, low / len(pieces), top_value / len(pieces))
        gain = gain * jnp.repeat(jnp.exp(draws), shape[position] // parts).reshape((-1,) + (1,) * (len(shape) - 1 - position))
    return gain


def shared_out(stream_key, own, number, rows, amount, top, most, lean):
    ranking = jax.random.permutation(stream_key, amount)
    heavy_load, usual = shares(amount, rows * top, most, lean, True), shares(amount, rows * top, most, lean, False)
    places = jnp.arange(amount)

    def named(sizes, offset_by):
        used = int((sizes > 0).sum())
        fixed = max(1, used // 4)
        passed = fixed + (places - fixed + offset_by * (used - fixed)) % max(1, amount - fixed)
        return jnp.zeros((amount,), jnp.int32).at[ranking[jnp.where(places < fixed, places, passed)]].set(jnp.asarray(sizes, jnp.int32))

    sizes = jnp.where(number % 4 == 0, named(heavy_load, number // 4), named(usual, number - number // 4 - 1))
    mixed = jax.random.permutation(jax.random.fold_in(own, 3), amount)
    giver, taker = mixed[0:amount // 2 * 2:2], mixed[1:amount // 2 * 2:2]
    room = jnp.minimum(sizes[giver] - 1, most - sizes[taker]) // 2
    room = jnp.where((giver == ranking[0]) | (taker == ranking[0]) | (sizes[taker] == 0), 0, jnp.maximum(room, 0))
    passed = jax.random.randint(jax.random.fold_in(own, 4), (amount // 2,), 0, 1 << 20) % (room + 1)
    sizes = sizes.at[giver].add(-passed).at[taker].add(passed)
    labels = jnp.searchsorted(jnp.cumsum(sizes), jnp.arange(rows * top), side="right").astype(jnp.int32)
    table = labels.reshape(top, rows).T
    table = table[jax.random.permutation(jax.random.fold_in(own, 1), rows)]
    offset_by = jax.random.randint(jax.random.fold_in(own, 2), (rows, 1), 0, top)
    return jnp.take_along_axis(table, (jnp.arange(top)[None, :] + offset_by) % top, axis=1)


def shares(count, total, most, lean, full):
    portions = [(1 << 20) // math.isqrt(rank ** lean) + 1 for rank in range(1, count + 1)]
    largest = most if full else min(most, max(-(-total // count), total * portions[0] // sum(portions)))
    least = 1 if total - largest >= count - 1 else 0
    counts, spare = [largest] + [least] * (count - 1), total - largest - least * (count - 1)
    while spare > 0:
        free = [i for i in range(1, count) if counts[i] < largest] or [i for i in range(1, count) if counts[i] < most]
        pool, remaining = sum([portions[i] for i in free]), spare
        for i in free:
            extra = min(most - counts[i], max(1, remaining * portions[i] // pool), spare)
            counts[i] = counts[i] + extra
            spare = spare - extra
    return np.array(counts)


def normal_values(stream_key, shape, scale, most, cuts=(), kind=jnp.bfloat16):
    array = scale * jax.random.normal(stream_key, shape, jnp.float32)
    if cuts:
        array = array * levels(stream_key, shape, cuts, -0.22, 0.18)
    return jnp.clip(array, -most, most).astype(kind)


def setup_inputs(seed: int = 0) -> dict:
    splits = jax.random.split(jax.random.key(seed), 9)
    queries = draw_queries(jax.random.fold_in(splits[8], 71), 0)
    latent_key_cache = draw_latent_key_cache(jax.random.fold_in(splits[8], 71), 0)
    cache_lengths = draw_cache_lengths(jax.random.fold_in(splits[8], 71), 0)
    token_rows = normal_values(splits[3], (TOKENS, D), 1.0, 6.0, ((0, 64),))
    expert_ids_keys = jax.random.split(jax.random.fold_in(splits[4], 1), TOKENS // ROWS_DEV)
    expert_ids_turns = jax.random.permutation(jax.random.fold_in(splits[4], 3), TOKENS // ROWS_DEV)
    expert_ids = jax.vmap(lambda own, number: shared_out(jax.random.fold_in(splits[4], 2), own, number, ROWS_DEV, EXPERTS, TOP, CAPD, 2))(expert_ids_keys, expert_ids_turns).reshape((TOKENS, TOP))
    gate_scores = jnp.clip(jnp.exp(math.log(1.0) - 2.3025851 * jax.random.uniform(splits[5], (TOKENS, TOP), jnp.float32) ** levels(splits[5], (TOKENS, TOP), ((0, 64),), -0.2, 0.2)), 0.1, 1.0)
    up_maps = normal_values(splits[6], (EXPERTS, D, FF_HID), D ** -0.5, 0.0625, ((0, 64), (2, 8)))
    down_maps = normal_values(splits[7], (EXPERTS, FF_HID, D), FF_HID ** -0.5, 0.1875, ((0, 64), (1, 8)))
    return {"queries": queries, "latent_key_cache": latent_key_cache, "cache_lengths": cache_lengths, "token_rows": token_rows, "expert_ids": expert_ids, "gate_scores": gate_scores, "up_maps": up_maps, "down_maps": down_maps}


SCALE = 192.0 ** -0.5
NEGATIVE = -1e30
ROUTE_SCALE = 2.5


def join_partials(earlier, latter):
    max_one, sum_one, val_one = earlier
    max_two, sum_two, val_two = latter
    joint_max = jnp.maximum(max_one, max_two)
    factor_one = jnp.exp(max_one - joint_max)
    factor_two = jnp.exp(max_two - joint_max)
    return (joint_max, sum_one * factor_one + sum_two * factor_two,
            val_one * factor_one[..., None] + val_two * factor_two[..., None])


def attend_one(packed):
    query_seq, cache_seq, length = packed
    block_len = NCTX // N_CTX
    step_total = query_seq.shape[0]
    head_total = query_seq.shape[2]
    key_limit = length - (step_total - 1 - jnp.arange(step_total, dtype=jnp.int32))

    def one_block(carry, block_index):
        cache_block = lax.dynamic_slice_in_dim(cache_seq, (block_index * block_len).astype(jnp.int32), block_len, 1)
        positions = block_index * block_len + jnp.arange(block_len, dtype=jnp.int32)
        scores = jnp.einsum('tdh,dl->thl', query_seq.astype(jnp.float32), cache_block.astype(jnp.float32),
                            precision=lax.Precision.HIGHEST) * SCALE
        live_keys = positions[None, None, :] < key_limit[:, None, None]
        block_max = jnp.max(jnp.where(live_keys, scores, NEGATIVE), axis=2)
        weights = jnp.where(live_keys, jnp.exp(scores - block_max[..., None]), 0.0)
        weight_sum = jnp.sum(weights, axis=2)
        rounded_length = lax.optimization_barrier(weights.astype(jnp.bfloat16)).astype(jnp.float32)
        block_value_rows = jnp.einsum('zmu,eu->zme', rounded_length, cache_block[:LATENT_RANK].astype(jnp.float32),
                                  precision=lax.Precision.HIGHEST)
        return join_partials(carry, (block_max, weight_sum, block_value_rows)), None

    start = (jnp.full((step_total, head_total), NEGATIVE, jnp.float32),
             jnp.zeros((step_total, head_total), jnp.float32),
             jnp.zeros((step_total, head_total, LATENT_RANK), jnp.float32))
    (joint_max, weight_sum, accum), _ = lax.scan(one_block, start, jnp.arange(N_CTX, dtype=jnp.int32))
    return (accum / weight_sum[..., None]).astype(jnp.bfloat16)


def reference(queries, latent_key_cache, cache_lengths, token_rows, expert_ids, gate_scores, up_maps, down_maps):
    attended = lax.map(attend_one, (queries, latent_key_cache, cache_lengths))

    gate_values = (gate_scores / jnp.sum(gate_scores, axis=1, keepdims=True) * ROUTE_SCALE).astype(jnp.bfloat16)
    flat_ids = expert_ids.reshape(-1).astype(jnp.int32)
    flat_gates = gate_values.reshape(-1).astype(jnp.float32)
    bound = N_EXP * CAPD
    slice_len = FF_HID // N_CTX

    def one_expert(total, packed):
        up_one, down_one, expert = packed
        hits = flat_ids == expert
        count = jnp.sum(hits.astype(jnp.int32))
        picks = jnp.nonzero(hits, size=bound, fill_value=0)[0].astype(jnp.int32)
        valid = jnp.arange(bound, dtype=jnp.int32) < count
        row_index = (picks // TOP).astype(jnp.int32)
        rows = token_rows[row_index]
        inner = jax.nn.silu(jnp.dot(rows, up_one, preferred_element_type=jnp.float32)).astype(jnp.bfloat16)
        summed = jnp.zeros((bound, D), jnp.float32)
        for part in range(N_CTX):
            piece = jnp.dot(inner[:, part * slice_len:(part + 1) * slice_len],
                            down_one[part * slice_len:(part + 1) * slice_len],
                            preferred_element_type=jnp.float32)
            summed = summed + lax.optimization_barrier(piece.astype(jnp.bfloat16)).astype(jnp.float32)
        weight = jnp.where(valid, flat_gates[picks], 0.0)
        total = total.at[row_index].add(weight[:, None] * summed)
        return total, None

    total, _ = lax.scan(one_expert, jnp.zeros((TOKENS, D), jnp.float32),
                        (up_maps, down_maps, jnp.arange(EXPERTS, dtype=jnp.int32)))
    return attended, total.astype(jnp.bfloat16)
```

```python
import jax
import jax.numpy as jnp
from jax import lax
from jax.sharding import PartitionSpec as P

LATENT_RANK = 512


SCALE = 192.0 ** (-0.5)
NEGATIVE = -1e30
ROUTE_SCALE = 2.5


def shards(
    queries,
    latent_key_cache,
    cache_lengths,
    token_rows,
    expert_ids,
    gate_scores,
    up_maps,
    down_maps,
):
    step_total = queries.shape[1]
    key_span = latent_key_cache.shape[2]
    key_start = lax.axis_index("ctx") * key_span
    positions = key_start + jnp.arange(key_span, dtype=jnp.int32)
    scores = (
        jnp.einsum("stdh,sdl->sthl", queries, latent_key_cache, preferred_element_type=jnp.float32)
        * SCALE
    )
    key_limit = (
        cache_lengths[:, None] - (step_total - 1 - jnp.arange(step_total, dtype=jnp.int32))[None, :]
    )
    live_keys = positions[None, None, None, :] < key_limit[:, :, None, None]
    block_max = jnp.max(jnp.where(live_keys, scores, NEGATIVE), axis=3)
    weights = jnp.where(live_keys, jnp.exp(scores - block_max[..., None]), 0.0)
    weight_sum = jnp.sum(weights, axis=3)
    block_value_rows = jnp.einsum(
        "sthl,sdl->sthd",
        weights.astype(jnp.bfloat16),
        latent_key_cache[:, :LATENT_RANK, :],
        preferred_element_type=jnp.float32,
    )
    shares_n = lax.axis_size("ctx")
    own_heads = queries.shape[3] // shares_n

    def by_heads(part):
        split = part.reshape(part.shape[:2] + (shares_n, own_heads) + part.shape[3:])
        return jnp.moveaxis(split, 2, 0)

    stats = lax.all_to_all(by_heads(jnp.stack([block_max, weight_sum], axis=-1)), "ctx", 0, 0)
    block_values = lax.all_to_all(
        by_heads(block_value_rows.astype(jnp.bfloat16)), "ctx", 0, 0
    ).astype(jnp.float32)
    factors = jnp.exp(stats[..., 0] - jnp.max(stats[..., 0], axis=0))
    total = jnp.sum(stats[..., 1] * factors, axis=0)
    attended = (
        jnp.sum(block_values * factors[..., None], axis=0) / total[..., None]
    ).astype(jnp.bfloat16)
    rows_n, top_n = expert_ids.shape
    groups_n = lax.axis_size("exp")
    capacity = 2 * rows_n * top_n // groups_n
    slots_n = groups_n * capacity
    gate_values = (gate_scores / jnp.sum(gate_scores, axis=1, keepdims=True) * ROUTE_SCALE).astype(
        jnp.bfloat16
    )
    flat_group = expert_ids.reshape(-1)
    member = (flat_group[:, None] == jnp.arange(groups_n, dtype=jnp.int32)[None, :]).astype(
        jnp.int32
    )
    rank_in_group = jnp.sum((jnp.cumsum(member, axis=0) - 1) * member, axis=1)
    slot_index = flat_group * capacity + rank_in_group
    placed = slot_index[:, None] == jnp.arange(slots_n, dtype=jnp.int32)[None, :]
    placed_rows = placed.reshape(rows_n, top_n, slots_n).astype(jnp.bfloat16)
    width = token_rows.shape[1] // shares_n
    own_columns = lax.dynamic_slice_in_dim(token_rows, lax.axis_index("ctx") * width, width, 1)
    outgoing = jnp.einsum("rkj,rd->jd", placed_rows, own_columns, preferred_element_type=jnp.float32)
    outgoing = outgoing.astype(jnp.bfloat16).reshape(groups_n, capacity, -1)
    arrived = lax.all_to_all(outgoing, "exp", split_axis=0, concat_axis=0, tiled=True)
    arrived = lax.all_gather(arrived.reshape(slots_n, width), "ctx")
    inner = jnp.einsum(
        "xjd,xdq->jq",
        arrived,
        up_maps[0].reshape(shares_n, width, -1),
        preferred_element_type=jnp.float32,
    )
    inner = jax.nn.silu(inner).astype(jnp.bfloat16)
    part_out = jnp.einsum("jq,qd->jd", inner, down_maps[0], preferred_element_type=jnp.float32)
    summed = lax.psum_scatter(
        part_out.astype(jnp.bfloat16), "ctx", scatter_dimension=1, tiled=True
    )
    returned = lax.all_to_all(
        summed.reshape(groups_n, capacity, width), "exp", split_axis=0, concat_axis=0, tiled=True
    )
    gate_table = placed_rows * gate_values[:, :, None]
    combined = jnp.einsum(
        "rkj,jd->rd", gate_table, returned.reshape(slots_n, -1), preferred_element_type=jnp.float32
    ).astype(jnp.bfloat16)
    return (attended, combined)


def solution(mesh):
    in_specs = (
        P("exp", None, None, None),
        P("exp", None, "ctx"),
        P("exp"),
        P("exp", None),
        P("exp", None),
        P("exp", None),
        P("exp", None, "ctx"),
        P("exp", "ctx", None),
    )
    out_specs = (P("exp", None, "ctx", None), P("exp", "ctx"))
    return jax.shard_map(shards, mesh=mesh, in_specs=in_specs, out_specs=out_specs, check_vma=False)
```

```python
import functools

import jax
import jax.numpy as jnp
from jax import lax
from jax.experimental import pallas as pl
from jax.experimental.pallas import tpu as pltpu
from jax.sharding import PartitionSpec as P

MESH = pl.DeviceIdType.MESH
BF16, F32 = jnp.bfloat16, jnp.float32

SCALE = 192.0 ** (-0.5)
NEGATIVE = -1e30
ROUTE_SCALE = 2.5

NX, NY, NZ = 4, 4, 16
ROWS = 16
CAP = 4
WIDTH = 896
TABLE = 128
LATENT = 512
KEYS = 512
HEADS = 128
OWN_HEADS = 16
CLASSES = (0, 1, 3, 2)
SPLIT = 512
SLOTS = 4 * ROWS


def nt(a, b):
    return lax.dot_general(a, b, (((1,), (1,)), ((), ())), preferred_element_type=F32)


def tn(a, b):
    return lax.dot_general(a, b, (((0,), (0,)), ((), ())), preferred_element_type=F32)


def nn(a, b):
    return jnp.dot(a, b, preferred_element_type=F32)


def kernel(
    n_send,
    queries,
    cache,
    lengths,
    tokens,
    ids,
    gates,
    up,
    down,
    attended,
    combined,
    query_v,
    cache_v,
    up_v,
    down_v,
    rows_v,
    picked_v,
    gate_v,
    gathered_v,
    part_v,
    part_in,
    far_a,
    far_b,
    far_a_in,
    far_b_in,
    own_f,
    near_f,
    near_v,
    near_in,
    back_v,
    back_in,
    comb_v,
    comb_in,
    comb2a_in,
    comb2b_in,
    zsum,
    zfar_a,
    zfar_b,
    zfar_a_in,
    zfar_b_in,
    znear,
    znear_in,
    att_v,
    att_s,
    att_v_in,
    att_s_in,
    load_sem,
    send_sem,
    recv_sem,
):
    ctx, exp = lax.axis_index("ctx"), lax.axis_index("exp")
    x, core = ctx // 2, ctx % 2
    z, y = exp // NY, exp % NY
    sent = []

    def along_x(step):
        return (2 * ((x + step + NX) % NX) + core, exp)

    def along_y(step):
        return (ctx, NY * z + (y + step) % NY)

    def along_z(step):
        return (ctx, NY * ((z + step + NZ) % NZ) + y)

    sibling = (2 * x + 1 - core, exp)

    def send(src, dst, device):
        copy = pltpu.make_async_remote_copy(
            src_ref=src,
            dst_ref=dst,
            send_sem=send_sem.at[len(sent)],
            recv_sem=recv_sem.at[len(sent)],
            device_id=device,
            device_id_type=MESH,
        )
        copy.start()
        sent.append(copy)
        return copy

    loads = []

    def load(src, dst):
        copy = pltpu.make_async_copy(src, dst, load_sem.at[len(loads)])
        copy.start()
        loads.append(copy)
        return copy

    token_load = load(
        tokens.at[:, pl.ds(pl.multiple_of(ctx * WIDTH, 128), WIDTH)],
        rows_v.at[0, pl.ds(0, ROWS), pl.ds(0, WIDTH)],
    )
    query_load = load(queries.at[0], query_v)
    cache_load = load(cache.at[0], cache_v)
    weight_loads = []
    for r in range(NX):
        piece = pl.multiple_of((2 * ((x + r) % NX) + core) * WIDTH, 128)
        weight_loads.append(
            load(up.at[0, pl.ds(piece, WIDTH), :], up_v.at[r, :, pl.ds(0, 128)])
        )
        weight_loads.append(
            load(down.at[0, :, pl.ds(piece, WIDTH)], down_v.at[r, pl.ds(0, 128), :])
        )

    partners = [((ctx + d) % 8, exp) for d in range(1, 8)]
    partners += [along_y(d) for d in (1, 2, 3)]
    partners += [along_z(d) for d in (1, -1, 2, -2, 4, -4)]
    barrier = pltpu.get_barrier_semaphore()
    for partner in partners:
        pl.semaphore_signal(barrier, inc=1, device_id=partner, device_id_type=MESH)

    scores = gates[...]
    values = (scores / jnp.sum(scores, axis=1, keepdims=True) * ROUTE_SCALE).astype(BF16)
    values = values.astype(F32)
    chosen = ids[...]
    lane = lax.broadcasted_iota(jnp.int32, (ROWS, TABLE), 1)
    table = jnp.zeros((ROWS, TABLE), F32)
    for k in range(chosen.shape[1]):
        table = table + jnp.where(chosen[:, k : k + 1] == lane, values[:, k : k + 1], 0.0)
    rows_v[0, 0:ROWS, WIDTH:] = table.astype(BF16)
    token_load.wait()
    pl.semaphore_wait(barrier, len(partners))

    def block(c, i, lanes=None):
        i = i % 4
        if lanes is None:
            return rows_v.at[c, pl.ds(i * ROWS, ROWS), :]
        return rows_v.at[c, pl.ds(i * ROWS, ROWS), pl.ds(*lanes)]

    arrivals = {0: [], 1: [], 2: [], 3: []}

    def forward(i):
        arrivals[1].append(send(block(0, i), block(1, i), along_z(-1)))
        arrivals[3].append(send(block(0, i), block(3, i - 1), along_z(1)))
        if i in (0, 3):
            arrivals[2].append(send(block(0, i), block(2, i - 1), along_z(2)))
        if i in (0, 1):
            arrivals[2].append(send(block(0, i), block(2, i), along_z(-2)))

    from_low = send(block(0, 0), block(0, 3), along_z(4))
    from_high = send(block(0, 0), block(0, 1), along_z(-4))
    forward(0)

    weight_copies = []
    for r in range(NX):
        piece = pl.multiple_of((2 * ((x + r) % NX) + 1 - core) * WIDTH, 128)
        weight_copies.append(
            send(up.at[0, pl.ds(piece, WIDTH), :], up_v.at[r, :, pl.ds(128, 128)], sibling)
        )
        weight_copies.append(
            send(
                down.at[0, :, pl.ds(piece, WIDTH)], down_v.at[r, pl.ds(128, 128), :], sibling
            )
        )

    def attend(t):
        score = tn(query_v[t], cache_v[...]) * SCALE
        position = ctx * KEYS + lax.broadcasted_iota(jnp.int32, (HEADS, KEYS), 1)
        live = position < lengths[0] - (1 - t)
        top = jnp.max(jnp.where(live, score, NEGATIVE), axis=1, keepdims=True)
        weight = jnp.where(live, jnp.exp(score - top), 0.0)
        total = jnp.sum(weight, axis=1, keepdims=True)
        value = nt(weight.astype(BF16), cache_v[0:LATENT, :])
        att_v[t] = value.astype(BF16)
        half = lax.broadcasted_iota(jnp.int32, (HEADS, 128), 1) < 64
        att_s[t] = jnp.where(half, top, total)

    query_load.wait()
    cache_load.wait()
    attend(0)
    from_low.wait_recv()
    arrivals[0].append(send(block(0, 3, (SPLIT, 512)), block(0, 2, (SPLIT, 512)), along_z(4)))
    forward(3)
    from_high.wait_recv()
    arrivals[0].append(send(block(0, 1, (0, SPLIT)), block(0, 2, (0, SPLIT)), along_z(-4)))
    forward(1)
    attend(1)
    heads_copies = []
    for d in range(1, 8):
        other = (ctx + d) % 8
        heads = pl.ds(pl.multiple_of(other * OWN_HEADS, OWN_HEADS), OWN_HEADS)
        heads_copies.append(send(att_v.at[:, heads, :], att_v_in.at[d - 1], (other, exp)))
        heads_copies.append(send(att_s.at[:, heads, :], att_s_in.at[d - 1], (other, exp)))
    for copy in arrivals[0]:
        copy.wait_recv()
    forward(2)

    def attend_join():
        for copy in heads_copies:
            copy.wait_recv()
        heads = pl.ds(pl.multiple_of(ctx * OWN_HEADS, OWN_HEADS), OWN_HEADS)
        for t in range(2):
            stats = [att_s[t, heads, :]] + [att_s_in[d, t] for d in range(7)]
            parts = [att_v[t, heads, :]] + [att_v_in[d, t] for d in range(7)]
            top = functools.reduce(jnp.maximum, [s[:, 0:1] for s in stats])
            factors = [jnp.exp(s[:, 0:1] - top) for s in stats]
            total = sum(s[:, 64:65] * f for s, f in zip(stats, factors))
            accum = sum(p.astype(F32) * f for p, f in zip(parts, factors))
            attended[0, t] = (accum / total).astype(BF16)

    slot = lax.broadcasted_iota(jnp.int32, (SLOTS, SLOTS), 1)
    row = lax.broadcasted_iota(jnp.int32, (SLOTS, SLOTS), 0)
    same_block = (row // ROWS) == (slot % ROWS) // CAP
    slot_rank = (slot % CAP).astype(F32)
    earlier = jnp.where((row // ROWS == slot // ROWS) & (slot < row), 1.0, 0.0).astype(BF16)
    expert_lane = lax.broadcasted_iota(jnp.int32, (TABLE, SLOTS), 0)
    expert_slot = lax.broadcasted_iota(jnp.int32, (TABLE, SLOTS), 1)
    spread = jnp.where(
        expert_lane == NY * z + (y + expert_slot // ROWS) % NY, 1.0, 0.0
    ).astype(BF16)

    y_copies, x_copies, x_relays, core_copies = {}, {}, {}, {}
    far_copies, near_copies, back_copies, comb_copies = {}, {}, {}, {}

    def select(c):
        if c:
            for copy in arrivals[c]:
                copy.wait_recv()
        gate = rows_v[c, :, WIDTH:]
        named = jnp.where(gate.astype(F32) > 0, 1.0, 0.0).astype(BF16)
        rank = nn(earlier, named).astype(BF16)
        here = nn(named, spread)
        rank_here = nn(rank, spread)
        gate_here = nn(gate, spread)
        hit = (here > 0.5) & (rank_here == slot_rank) & same_block
        gate_v[c] = jnp.where(hit, gate_here, 0.0).astype(BF16)
        picked = tn(jnp.where(hit, 1.0, 0.0).astype(BF16), rows_v[c, :, 0:WIDTH]).astype(BF16)
        picked_v[c] = picked
        gathered_v[c, 0, 0:ROWS, :] = picked[0:ROWS]
        y_copies[c] = [
            send(
                picked_v.at[c, pl.ds(d * ROWS, ROWS), :],
                gathered_v.at[c, 0, pl.ds((NY - d) * ROWS, ROWS), :],
                along_y(d),
            )
            for d in (1, 2, 3)
        ]

    def gather(c):
        for copy in y_copies[c]:
            copy.wait_recv()
        x_copies[c] = (
            send(gathered_v.at[c, 0], gathered_v.at[c, 3], along_x(1)),
            send(gathered_v.at[c, 0], gathered_v.at[c, 1], along_x(-1)),
        )

    def relay(c):
        x_copies[c][0].wait_recv()
        low = send(
            gathered_v.at[c, 3, :, pl.ds(0, SPLIT)],
            gathered_v.at[c, 2, :, pl.ds(0, SPLIT)],
            along_x(1),
        )
        x_copies[c][1].wait_recv()
        high = send(
            gathered_v.at[c, 1, :, pl.ds(SPLIT, WIDTH - SPLIT)],
            gathered_v.at[c, 2, :, pl.ds(SPLIT, WIDTH - SPLIT)],
            along_x(-1),
        )
        x_relays[c] = (low, high)

    def inner_part(c):
        if c == CLASSES[0]:
            for copy in weight_loads:
                copy.wait()
            for copy in weight_copies:
                copy.wait_recv()
        part = nn(gathered_v[c, 0], up_v[0])
        part = part + nn(gathered_v[c, 1], up_v[1])
        part = part + nn(gathered_v[c, 3], up_v[3])
        for copy in x_relays[c]:
            copy.wait_recv()
        part_v[c] = part + nn(gathered_v[c, 2], up_v[2])
        core_copies[c] = send(part_v.at[c], part_in.at[c], sibling)

    def outer_part(c):
        core_copies[c].wait_recv()
        total = part_v[c] + jnp.concatenate(
            [part_in[c, :, 128:256], part_in[c, :, 0:128]], axis=1
        )
        inner = (total / (1.0 + jnp.exp(-total))).astype(BF16)
        far = nn(inner, down_v[2]).astype(BF16)
        far_a[c] = far[:, 0:SPLIT]
        far_b[c] = far[:, SPLIT:]
        far_copies[c] = (
            send(far_a.at[c], far_a_in.at[c], along_x(1)),
            send(far_b.at[c], far_b_in.at[c], along_x(-1)),
        )
        near_f[0] = nn(inner, down_v[1])
        near_f[1] = nn(inner, down_v[3])
        own_f[c] = nn(inner, down_v[0])

    def join_far(c):
        far_copies[c][0].wait_recv()
        near_v[c, 0, :, 0:SPLIT] = (near_f[0, :, 0:SPLIT] + far_a_in[c].astype(F32)).astype(BF16)
        near_v[c, 0, :, SPLIT:] = near_f[0, :, SPLIT:].astype(BF16)
        up_copy = send(near_v.at[c, 0], near_in.at[c, 0], along_x(1))
        far_copies[c][1].wait_recv()
        near_v[c, 1, :, 0:SPLIT] = near_f[1, :, 0:SPLIT].astype(BF16)
        near_v[c, 1, :, SPLIT:] = (near_f[1, :, SPLIT:] + far_b_in[c].astype(F32)).astype(BF16)
        near_copies[c] = (up_copy, send(near_v.at[c, 1], near_in.at[c, 1], along_x(-1)))

    def join_near(c):
        for copy in near_copies[c]:
            copy.wait_recv()
        total = (own_f[c] + near_in[c, 0].astype(F32) + near_in[c, 1].astype(F32)).astype(BF16)
        back_v[c] = total
        back_in[c, 0:ROWS, :] = total[0:ROWS]
        back_copies[c] = [
            send(
                back_v.at[c, pl.ds(d * ROWS, ROWS), :],
                back_in.at[c, pl.ds((NY - d) * ROWS, ROWS), :],
                along_y(d),
            )
            for d in (1, 2, 3)
        ]

    def combine(c):
        for copy in back_copies[c]:
            copy.wait_recv()
        total = nn(gate_v[c], back_in[c])
        if c == 0:
            zsum[...] = total
            return
        comb_v[c - 1] = total.astype(BF16)
        half = 2 * ROWS
        if c == 1:
            comb_copies[1] = send(comb_v.at[0], comb_in.at[0], along_z(1))
        if c == 3:
            comb_copies[3] = send(comb_v.at[2], comb_in.at[1], along_z(-1))
        if c == 2:
            comb_copies[2] = (
                send(comb_v.at[1, pl.ds(0, half), :], comb2a_in, along_z(2)),
                send(comb_v.at[1, pl.ds(half, half), :], comb2b_in, along_z(-2)),
            )

    stages = (select, gather, relay, inner_part, outer_part, join_far, join_near, combine)
    for step in range(len(CLASSES) + len(stages) - 1):
        for s in reversed(range(len(stages))):
            if 0 <= step - s < len(CLASSES):
                stages[s](CLASSES[step - s])
        if step == 2:
            attend_join()

    def place(i):
        return pl.ds((i % 4) * ROWS, ROWS)

    comb_copies[1].wait_recv()
    comb_copies[3].wait_recv()
    totals = []
    for i in range(4):
        low = comb_in[0, i * ROWS : (i + 1) * ROWS, :].astype(F32)
        j = (i + 3) % 4
        high = comb_in[1, j * ROWS : (j + 1) * ROWS, :].astype(F32)
        totals.append(zsum[i * ROWS : (i + 1) * ROWS, :] + low + high)
    across = totals[2].astype(BF16)
    zfar_a[...] = across[:, 0:SPLIT]
    zfar_b[...] = across[:, SPLIT:]
    far_up = send(zfar_a, zfar_a_in, along_z(4))
    far_down = send(zfar_b, zfar_b_in, along_z(-4))
    for copy in comb_copies[2]:
        copy.wait_recv()
    totals[0] = totals[0] + comb2a_in[0:ROWS, :].astype(F32) + comb2b_in[ROWS:, :].astype(F32)
    totals[1] = totals[1] + comb2a_in[ROWS:, :].astype(F32)
    totals[3] = totals[3] + comb2b_in[0:ROWS, :].astype(F32)
    far_up.wait_recv()
    znear[0, :, 0:SPLIT] = (totals[1][:, 0:SPLIT] + zfar_a_in[...].astype(F32)).astype(BF16)
    znear[0, :, SPLIT:] = totals[1][:, SPLIT:].astype(BF16)
    near_up = send(znear.at[0], znear_in.at[0], along_z(4))
    far_down.wait_recv()
    znear[1, :, 0:SPLIT] = totals[3][:, 0:SPLIT].astype(BF16)
    znear[1, :, SPLIT:] = (totals[3][:, SPLIT:] + zfar_b_in[...].astype(F32)).astype(BF16)
    near_down = send(znear.at[1], znear_in.at[1], along_z(-4))
    near_up.wait_recv()
    near_down.wait_recv()
    combined[...] = (totals[0] + znear_in[0].astype(F32) + znear_in[1].astype(F32)).astype(BF16)

    for copy in sent:
        copy.wait_send()
    assert len(sent) == n_send, len(sent)


N_SEND = 106


def shards(queries, cache, lengths, tokens, ids, gates, up, down):
    vmem = pl.BlockSpec(memory_space=pltpu.VMEM)
    hbm = pl.BlockSpec(memory_space=pl.ANY)
    smem = pl.BlockSpec(memory_space=pltpu.SMEM)
    n_classes = len(CLASSES)

    def buf(*shape, dtype=BF16):
        return pltpu.VMEM(shape, dtype)

    return pl.pallas_call(
        functools.partial(kernel, N_SEND),
        out_shape=(
            jax.ShapeDtypeStruct((1, 2, OWN_HEADS, LATENT), BF16),
            jax.ShapeDtypeStruct((ROWS, WIDTH), BF16),
        ),
        in_specs=[hbm, hbm, smem, hbm, vmem, vmem, hbm, hbm],
        out_specs=(vmem, vmem),
        scratch_shapes=[
            buf(2, 576, HEADS),
            buf(576, KEYS),
            buf(NX, WIDTH, 256),
            buf(NX, 256, WIDTH),
            buf(n_classes, SLOTS, WIDTH + TABLE),
            buf(n_classes, SLOTS, WIDTH),
            buf(n_classes, SLOTS, SLOTS),
            buf(n_classes, NX, SLOTS, WIDTH),
            buf(n_classes, SLOTS, 256, dtype=F32),
            buf(n_classes, SLOTS, 256, dtype=F32),
            buf(n_classes, SLOTS, SPLIT),
            buf(n_classes, SLOTS, WIDTH - SPLIT),
            buf(n_classes, SLOTS, SPLIT),
            buf(n_classes, SLOTS, WIDTH - SPLIT),
            buf(n_classes, SLOTS, WIDTH, dtype=F32),
            buf(2, SLOTS, WIDTH, dtype=F32),
            buf(n_classes, 2, SLOTS, WIDTH),
            buf(n_classes, 2, SLOTS, WIDTH),
            buf(n_classes, SLOTS, WIDTH),
            buf(n_classes, SLOTS, WIDTH),
            buf(3, SLOTS, WIDTH),
            buf(2, SLOTS, WIDTH),
            buf(2 * ROWS, WIDTH),
            buf(2 * ROWS, WIDTH),
            buf(SLOTS, WIDTH, dtype=F32),
            buf(ROWS, SPLIT),
            buf(ROWS, WIDTH - SPLIT),
            buf(ROWS, SPLIT),
            buf(ROWS, WIDTH - SPLIT),
            buf(2, ROWS, WIDTH),
            buf(2, ROWS, WIDTH),
            buf(2, HEADS, LATENT),
            buf(2, HEADS, 128, dtype=F32),
            buf(7, 2, OWN_HEADS, LATENT),
            buf(7, 2, OWN_HEADS, 128, dtype=F32),
            pltpu.SemaphoreType.DMA((11,)),
            pltpu.SemaphoreType.DMA((N_SEND,)),
            pltpu.SemaphoreType.DMA((N_SEND,)),
        ],
        compiler_params=pltpu.CompilerParams(
            collective_id=0, has_side_effects=True, vmem_limit_bytes=40 * 1024 * 1024
        ),
    )(queries, cache, lengths, tokens, ids, gates, up, down)


def solution(mesh):
    in_specs = (
        P("exp", None, None, None),
        P("exp", None, "ctx"),
        P("exp"),
        P("exp", None),
        P("exp", None),
        P("exp", None),
        P("exp", None, "ctx"),
        P("exp", "ctx", None),
    )
    out_specs = (P("exp", None, "ctx", None), P("exp", "ctx"))
    return jax.shard_map(shards, mesh=mesh, in_specs=in_specs, out_specs=out_specs, check_vma=False)
```

```python
import functools

import jax
import jax.numpy as jnp
from jax import lax
from jax.experimental import pallas as pl
from jax.experimental.pallas import tpu as pltpu
from jax.sharding import PartitionSpec as P

MESH = pl.DeviceIdType.MESH
BF16, F32 = jnp.bfloat16, jnp.float32

SCALE = 192.0 ** (-0.5)
NEGATIVE = -1e30
ROUTE_SCALE = 2.5

NX, NY, NZ = 4, 4, 16
ROWS = 16
CAP = 4
WIDTH = 896
TABLE = 128
LATENT = 512
KEYS = 512
HEADS = 128
OWN_HEADS = 16
CLASSES = (0, 1, 3, 2)
BACK = (1, 3, 2, 0)
SPLITS = {1: 512, 3: 384, 2: 512, 0: 384}
UNITS = 128
SLOTS = 4 * ROWS


def nt(a, b):
    return lax.dot_general(a, b, (((1,), (1,)), ((), ())), preferred_element_type=F32)


def tn(a, b):
    return lax.dot_general(a, b, (((0,), (0,)), ((), ())), preferred_element_type=F32)


def nn(a, b):
    return jnp.dot(a, b, preferred_element_type=F32)


def kernel(
    n_send,
    queries,
    cache,
    lengths,
    tokens,
    ids,
    gates,
    up,
    down,
    attended,
    combined,
    query_v,
    cache_v,
    up_v,
    down_v,
    rows_v,
    picked_v,
    gate_v,
    gathered_v,
    part_v,
    part_in,
    own_part,
    inner_v,
    inner_in,
    far_v,
    far_in,
    own_f,
    near_f,
    near_v,
    near_in,
    back_v,
    back_in,
    comb_v,
    comb_in,
    comb2a_in,
    comb2b_in,
    zsum,
    zsend,
    zsend_in,
    att_v,
    att_s,
    att_v_in,
    att_s_in,
    load_sem,
    send_sem,
    recv_sem,
):
    ctx, exp = lax.axis_index("ctx"), lax.axis_index("exp")
    x, core = ctx // 2, ctx % 2
    z, y = exp // NY, exp % NY
    sent = []

    def along_x(step):
        return (2 * ((x + step + NX) % NX) + core, exp)

    def along_y(step):
        return (ctx, NY * z + (y + step) % NY)

    def along_z(step):
        return (ctx, NY * ((z + step + NZ) % NZ) + y)

    sibling = (2 * x + 1 - core, exp)

    def send(src, dst, device):
        copy = pltpu.make_async_remote_copy(
            src_ref=src,
            dst_ref=dst,
            send_sem=send_sem.at[len(sent)],
            recv_sem=recv_sem.at[len(sent)],
            device_id=device,
            device_id_type=MESH,
        )
        copy.start()
        sent.append(copy)
        return copy

    loads = []

    def load(src, dst):
        copy = pltpu.make_async_copy(src, dst, load_sem.at[len(loads)])
        copy.start()
        loads.append(copy)
        return copy

    token_load = load(
        tokens.at[:, pl.ds(pl.multiple_of(ctx * WIDTH, 128), WIDTH)],
        rows_v.at[0, pl.ds(0, ROWS), pl.ds(0, WIDTH)],
    )

    partners = [along_z(d) for d in (4, -4, 8, 1, -1, 2, -2)]
    partners += [along_y(d) for d in (1, 2, 3)]
    partners += [((ctx + d) % 8, exp) for d in range(1, 8)]
    barrier = pltpu.get_barrier_semaphore()
    for partner in partners:
        pl.semaphore_signal(barrier, inc=1, device_id=partner, device_id_type=MESH)

    query_load = load(queries.at[0], query_v)
    cache_load = load(cache.at[0], cache_v)

    def up_rows(step, which):
        piece = 2 * ((x + step + NX) % NX) + (1 - core if which else core)
        return up.at[0, pl.ds(pl.multiple_of(piece * WIDTH, 128), WIDTH), :]

    def up_place(which, source):
        return up_v.at[which, :, pl.ds(source * UNITS, UNITS)]

    weight_loads = [load(up_rows(0, which), up_place(which, 0)) for which in (0, 1)]
    for r in range(NX):
        piece = pl.multiple_of((2 * ((x + r) % NX) + core) * WIDTH, 128)
        weight_loads.append(
            load(down.at[0, :, pl.ds(piece, WIDTH)], down_v.at[r, pl.ds(0, UNITS), :])
        )

    scores = gates[...]
    values = (scores / jnp.sum(scores, axis=0, keepdims=True) * ROUTE_SCALE).astype(BF16)
    values = values.astype(F32)
    chosen = ids[...]
    expert = lax.broadcasted_iota(jnp.int32, (TABLE, ROWS), 0)
    table = jnp.zeros((TABLE, ROWS), F32)
    for k in range(chosen.shape[0]):
        table = table + jnp.where(chosen[k : k + 1, :] == expert, values[k : k + 1, :], 0.0)
    unit_row = lax.broadcasted_iota(jnp.int32, (TABLE, TABLE), 0)
    unit_lane = lax.broadcasted_iota(jnp.int32, (TABLE, TABLE), 1)
    unit = jnp.where(unit_row == unit_lane, 1.0, 0.0).astype(BF16)
    rows_v[0, 0:ROWS, WIDTH:] = tn(table.astype(BF16), unit).astype(BF16)
    token_load.wait()
    pl.semaphore_wait(barrier, len(partners))

    def block(c, i):
        return rows_v.at[c, pl.ds(i % 4 * ROWS, ROWS), :]

    arrivals = {1: [], 2: [], 3: []}

    def forward(i):
        arrivals[1].append(send(block(0, i), block(1, i), along_z(-1)))
        arrivals[3].append(send(block(0, i), block(3, i - 1), along_z(1)))
        if i in (0, 3):
            arrivals[2].append(send(block(0, i), block(2, i - 1), along_z(2)))
        if i in (0, 1):
            arrivals[2].append(send(block(0, i), block(2, i), along_z(-2)))

    from_low = send(block(0, 0), block(0, 3), along_z(4))
    from_high = send(block(0, 0), block(0, 1), along_z(-4))
    from_far = send(block(0, 0), block(0, 2), along_z(8))
    forward(0)

    up_copies = []
    for step in (2, 1, -1):
        for which in (0, 1):
            up_copies.append(
                send(up_rows(step, which), up_place(which, (NX - step) % NX), along_x(step))
            )
    down_copies = []
    for r in range(NX):
        piece = pl.multiple_of((2 * ((x + r) % NX) + 1 - core) * WIDTH, 128)
        down_copies.append(
            send(
                down.at[0, :, pl.ds(piece, WIDTH)],
                down_v.at[r, pl.ds(UNITS, UNITS), :],
                sibling,
            )
        )

    def attend(t):
        score = tn(query_v[t], cache_v[...]) * SCALE
        position = ctx * KEYS + lax.broadcasted_iota(jnp.int32, (HEADS, KEYS), 1)
        live = position < lengths[0] - (1 - t)
        top = jnp.max(jnp.where(live, score, NEGATIVE), axis=1, keepdims=True)
        weight = jnp.where(live, jnp.exp(score - top), 0.0)
        total = jnp.sum(weight, axis=1, keepdims=True)
        value = nt(weight.astype(BF16), cache_v[0:LATENT, :])
        att_v[t] = value.astype(BF16)
        half = lax.broadcasted_iota(jnp.int32, (HEADS, 128), 1) < 64
        att_s[t] = jnp.where(half, top, total)

    query_load.wait()
    cache_load.wait()
    attend(0)
    from_low.wait_recv()
    forward(3)
    from_high.wait_recv()
    forward(1)
    from_far.wait_recv()
    forward(2)
    attend(1)

    heads_copies = []

    def attend_send():
        for d in range(1, 8):
            other = (ctx + d) % 8
            heads = pl.ds(pl.multiple_of(other * OWN_HEADS, OWN_HEADS), OWN_HEADS)
            heads_copies.append(send(att_v.at[:, heads, :], att_v_in.at[d - 1], (other, exp)))
            heads_copies.append(send(att_s.at[:, heads, :], att_s_in.at[d - 1], (other, exp)))

    def attend_join():
        for copy in heads_copies:
            copy.wait_recv()
        heads = pl.ds(pl.multiple_of(ctx * OWN_HEADS, OWN_HEADS), OWN_HEADS)
        for t in range(2):
            stats = [att_s[t, heads, :]] + [att_s_in[d, t] for d in range(7)]
            parts = [att_v[t, heads, :]] + [att_v_in[d, t] for d in range(7)]
            top = functools.reduce(jnp.maximum, [s[:, 0:1] for s in stats])
            factors = [jnp.exp(s[:, 0:1] - top) for s in stats]
            total = sum(s[:, 64:65] * f for s, f in zip(stats, factors))
            accum = sum(p.astype(F32) * f for p, f in zip(parts, factors))
            attended[0, t] = (accum / total).astype(BF16)

    slot = lax.broadcasted_iota(jnp.int32, (SLOTS, SLOTS), 1)
    row = lax.broadcasted_iota(jnp.int32, (SLOTS, SLOTS), 0)
    same_block = (row // ROWS) == (slot % ROWS) // CAP
    slot_rank = (slot % CAP).astype(F32)
    earlier = jnp.where((row // ROWS == slot // ROWS) & (slot < row), 1.0, 0.0).astype(BF16)
    expert_lane = lax.broadcasted_iota(jnp.int32, (TABLE, SLOTS), 0)
    expert_slot = lax.broadcasted_iota(jnp.int32, (TABLE, SLOTS), 1)
    spread = jnp.where(
        expert_lane == NY * z + (y + expert_slot // ROWS) % NY, 1.0, 0.0
    ).astype(BF16)

    y_copies, pair_copies, part_copies, inner_copies = {}, {}, {}, {}
    far_copies, near_copies, back_copies, comb_copies = {}, {}, {}, {}

    def select(c):
        if c:
            for copy in arrivals[c]:
                copy.wait_recv()
        gate = rows_v[c, :, WIDTH:]
        named = jnp.where(gate.astype(F32) > 0, 1.0, 0.0).astype(BF16)
        rank = nn(earlier, named).astype(BF16)
        here = nn(named, spread)
        rank_here = nn(rank, spread)
        gate_here = nn(gate, spread)
        hit = (here > 0.5) & (rank_here == slot_rank) & same_block
        gate_v[c] = jnp.where(hit, gate_here, 0.0).astype(BF16)
        picked = tn(jnp.where(hit, 1.0, 0.0).astype(BF16), rows_v[c, :, 0:WIDTH]).astype(BF16)
        picked_v[c] = picked
        first = BACK.index(c) * SLOTS
        gathered_v[0, first : first + ROWS, :] = picked[0:ROWS]
        y_copies[c] = [
            send(
                picked_v.at[c, pl.ds(d * ROWS, ROWS), :],
                gathered_v.at[0, pl.ds(first + (NY - d) * ROWS, ROWS), :],
                along_y(d),
            )
            for d in (1, 2, 3)
        ]

    def pair(c):
        for copy in y_copies[c]:
            copy.wait_recv()
        rows = pl.ds(BACK.index(c) * SLOTS, SLOTS)
        pair_copies[c] = send(gathered_v.at[0, rows, :], gathered_v.at[1, rows, :], sibling)

    def rows_of(b):
        return pl.ds(b * 2 * SLOTS, 2 * SLOTS)

    def inner_part(b):
        if b == 0:
            for copy in weight_loads:
                copy.wait()
            for copy in up_copies:
                copy.wait_recv()
        for c in BACK[2 * b : 2 * b + 2]:
            pair_copies[c].wait_recv()
        part = nn(gathered_v[0, rows_of(b), :], up_v[0])
        part = part + nn(gathered_v[1, rows_of(b), :], up_v[1])
        own_part[b] = part[:, 0:UNITS]
        part_copies[b] = []
        for r in (2, 1, 3):
            part_v[b, r - 1] = part[:, r * UNITS : (r + 1) * UNITS].astype(BF16)
            part_copies[b].append(send(part_v.at[b, r - 1], part_in.at[b, r - 1], along_x(r)))

    def inner_sum(b):
        for copy in part_copies[b]:
            copy.wait_recv()
        total = own_part[b] + part_in[b, 0].astype(F32)
        total = total + part_in[b, 1].astype(F32) + part_in[b, 2].astype(F32)
        inner_v[b] = (total / (1.0 + jnp.exp(-total))).astype(BF16)
        inner_copies[b] = send(inner_v.at[b], inner_in.at[b], sibling)

    def outer_part(b):
        if b == 0:
            for copy in down_copies:
                copy.wait_recv()
        inner_copies[b].wait_recv()
        inner = jnp.concatenate([inner_v[b], inner_in[b]], axis=1)
        far = nn(inner, down_v[2]).astype(BF16)
        for i, c in enumerate(BACK[2 * b : 2 * b + 2]):
            far_v[c] = far[i * SLOTS : (i + 1) * SLOTS]
            low, high = pl.ds(0, SPLITS[c]), pl.ds(SPLITS[c], WIDTH - SPLITS[c])
            far_copies[c] = (
                send(far_v.at[c, :, low], far_in.at[c, :, low], along_x(1)),
                send(far_v.at[c, :, high], far_in.at[c, :, high], along_x(-1)),
            )
        near_f[b, 0] = nn(inner, down_v[1])
        near_f[b, 1] = nn(inner, down_v[3])
        own_f[b] = nn(inner, down_v[0])

    def half_of(c):
        b, i = divmod(BACK.index(c), 2)
        return b, pl.ds(i * SLOTS, SLOTS)

    def join_far(c):
        split = SPLITS[c]
        b, rows = half_of(c)
        up_near, down_near = near_f[b, 0, rows, :], near_f[b, 1, rows, :]
        far_copies[c][0].wait_recv()
        near_v[c, 0, :, 0:split] = (
            up_near[:, 0:split] + far_in[c, :, 0:split].astype(F32)
        ).astype(BF16)
        near_v[c, 0, :, split:] = up_near[:, split:].astype(BF16)
        up_copy = send(near_v.at[c, 0], near_in.at[c, 0], along_x(1))
        far_copies[c][1].wait_recv()
        near_v[c, 1, :, 0:split] = down_near[:, 0:split].astype(BF16)
        near_v[c, 1, :, split:] = (
            down_near[:, split:] + far_in[c, :, split:].astype(F32)
        ).astype(BF16)
        near_copies[c] = (up_copy, send(near_v.at[c, 1], near_in.at[c, 1], along_x(-1)))

    def join_near(c):
        for copy in near_copies[c]:
            copy.wait_recv()
        b, rows = half_of(c)
        total = (own_f[b, rows, :] + near_in[c, 0].astype(F32) + near_in[c, 1].astype(F32)).astype(BF16)
        back_v[c] = total
        back_in[c, 0:ROWS, :] = total[0:ROWS]
        back_copies[c] = [
            send(
                back_v.at[c, pl.ds(d * ROWS, ROWS), :],
                back_in.at[c, pl.ds((NY - d) * ROWS, ROWS), :],
                along_y(d),
            )
            for d in (1, 2, 3)
        ]

    def combine(c):
        for copy in back_copies[c]:
            copy.wait_recv()
        total = nn(gate_v[c], back_in[c])
        if c == 0:
            zsum[...] = total
            return
        comb_v[c - 1] = total.astype(BF16)
        half = 2 * ROWS
        if c == 1:
            comb_copies[1] = send(comb_v.at[0], comb_in.at[0], along_z(1))
        if c == 3:
            comb_copies[3] = send(comb_v.at[2], comb_in.at[1], along_z(-1))
        if c == 2:
            comb_copies[2] = (
                send(comb_v.at[1, pl.ds(0, half), :], comb2a_in, along_z(2)),
                send(comb_v.at[1, pl.ds(half, half), :], comb2b_in, along_z(-2)),
            )

    select(0)
    select(1)
    pair(0)
    select(3)
    pair(1)
    select(2)
    pair(3)
    pair(2)
    inner_part(0)
    inner_part(1)
    attend_send()
    inner_sum(0)
    inner_sum(1)
    outer_part(0)
    outer_part(1)
    join_far(BACK[0])
    join_far(BACK[1])
    join_near(BACK[0])
    join_far(BACK[2])
    join_near(BACK[1])
    join_far(BACK[3])
    combine(BACK[0])
    attend_join()
    join_near(BACK[2])
    combine(BACK[1])
    join_near(BACK[3])
    combine(BACK[2])
    combine(BACK[3])

    comb_copies[1].wait_recv()
    comb_copies[3].wait_recv()
    totals = []
    for i in range(4):
        low = comb_in[0, i * ROWS : (i + 1) * ROWS, :].astype(F32)
        j = (i + 3) % 4
        high = comb_in[1, j * ROWS : (j + 1) * ROWS, :].astype(F32)
        totals.append(zsum[i * ROWS : (i + 1) * ROWS, :] + low + high)
    for copy in comb_copies[2]:
        copy.wait_recv()
    totals[0] = totals[0] + comb2a_in[0:ROWS, :].astype(F32) + comb2b_in[ROWS:, :].astype(F32)
    totals[1] = totals[1] + comb2a_in[ROWS:, :].astype(F32)
    totals[3] = totals[3] + comb2b_in[0:ROWS, :].astype(F32)
    last_copies = []
    for i in (2, 1, 3):
        zsend[i - 1] = totals[i].astype(BF16)
        last_copies.append(send(zsend.at[i - 1], zsend_in.at[i - 1], along_z(4 * i)))
    for copy in last_copies:
        copy.wait_recv()
    combined[...] = (
        totals[0]
        + zsend_in[0].astype(F32)
        + zsend_in[1].astype(F32)
        + zsend_in[2].astype(F32)
    ).astype(BF16)

    for copy in sent:
        copy.wait_send()
    assert len(sent) == n_send, len(sent)


N_SEND = 98


def shards(queries, cache, lengths, tokens, ids, gates, up, down):
    vmem = pl.BlockSpec(memory_space=pltpu.VMEM)
    hbm = pl.BlockSpec(memory_space=pl.ANY)
    smem = pl.BlockSpec(memory_space=pltpu.SMEM)
    n_classes = len(CLASSES)

    def buf(*shape, dtype=BF16):
        return pltpu.VMEM(shape, dtype)

    return pl.pallas_call(
        functools.partial(kernel, N_SEND),
        out_shape=(
            jax.ShapeDtypeStruct((1, 2, OWN_HEADS, LATENT), BF16),
            jax.ShapeDtypeStruct((ROWS, WIDTH), BF16),
        ),
        in_specs=[hbm, hbm, smem, hbm, vmem, vmem, hbm, hbm],
        out_specs=(vmem, vmem),
        scratch_shapes=[
            buf(2, 576, HEADS),
            buf(576, KEYS),
            buf(2, WIDTH, NX * UNITS),
            buf(NX, 256, WIDTH),
            buf(n_classes, SLOTS, WIDTH + TABLE),
            buf(n_classes, SLOTS, WIDTH),
            buf(n_classes, SLOTS, SLOTS),
            buf(2, n_classes * SLOTS, WIDTH),
            buf(2, 3, 2 * SLOTS, UNITS),
            buf(2, 3, 2 * SLOTS, UNITS),
            buf(2, 2 * SLOTS, UNITS, dtype=F32),
            buf(2, 2 * SLOTS, UNITS),
            buf(2, 2 * SLOTS, UNITS),
            buf(n_classes, SLOTS, WIDTH),
            buf(n_classes, SLOTS, WIDTH),
            buf(2, 2 * SLOTS, WIDTH, dtype=F32),
            buf(2, 2, 2 * SLOTS, WIDTH, dtype=F32),
            buf(n_classes, 2, SLOTS, WIDTH),
            buf(n_classes, 2, SLOTS, WIDTH),
            buf(n_classes, SLOTS, WIDTH),
            buf(n_classes, SLOTS, WIDTH),
            buf(3, SLOTS, WIDTH),
            buf(2, SLOTS, WIDTH),
            buf(2 * ROWS, WIDTH),
            buf(2 * ROWS, WIDTH),
            buf(SLOTS, WIDTH, dtype=F32),
            buf(3, ROWS, WIDTH),
            buf(3, ROWS, WIDTH),
            buf(2, HEADS, LATENT),
            buf(2, HEADS, 128, dtype=F32),
            buf(7, 2, OWN_HEADS, LATENT),
            buf(7, 2, OWN_HEADS, 128, dtype=F32),
            pltpu.SemaphoreType.DMA((9,)),
            pltpu.SemaphoreType.DMA((N_SEND,)),
            pltpu.SemaphoreType.DMA((N_SEND,)),
        ],
        compiler_params=pltpu.CompilerParams(
            collective_id=0, has_side_effects=True, vmem_limit_bytes=60 * 1024 * 1024
        ),
    )(queries, cache, lengths, tokens, ids.T, gates.T, up, down)


def solution(mesh):
    in_specs = (
        P("exp", None, None, None),
        P("exp", None, "ctx"),
        P("exp"),
        P("exp", None),
        P("exp", None),
        P("exp", None),
        P("exp", None, "ctx"),
        P("exp", "ctx", None),
    )
    out_specs = (P("exp", None, "ctx", None), P("exp", "ctx"))
    return jax.shard_map(shards, mesh=mesh, in_specs=in_specs, out_specs=out_specs, check_vma=False)
```

```python
import functools

import jax
import jax.numpy as jnp
from jax import lax
from jax.experimental import pallas as pl
from jax.experimental.pallas import tpu as pltpu
from jax.sharding import PartitionSpec as P

MESH = pl.DeviceIdType.MESH
BF16, F32 = jnp.bfloat16, jnp.float32

SCALE = 192.0 ** (-0.5)
NEGATIVE = -1e30
ROUTE_SCALE = 2.5

NX, NY, NZ = 4, 4, 16
ROWS = 16
CAP = 4
WIDTH = 896
TABLE = 128
LATENT = 512
KEYS = 512
HEADS = 128
OWN_HEADS = 16
CLASSES = (0, 1, 3, 2)
BACK = (1, 3, 2, 0)
SPLITS = {1: 384, 3: 512, 2: 384, 0: 512}
COLUMNS = {1: ((0, 896),), 3: ((0, 896),), 2: ((0, 896),), 0: ((0, 512), (512, 384))}
UNITS = 128
SLOTS = 4 * ROWS


def nt(a, b):
    return lax.dot_general(a, b, (((1,), (1,)), ((), ())), preferred_element_type=F32)


def tn(a, b):
    return lax.dot_general(a, b, (((0,), (0,)), ((), ())), preferred_element_type=F32)


def nn(a, b):
    return jnp.dot(a, b, preferred_element_type=F32)


def kernel(
    n_send,
    queries,
    cache,
    lengths,
    tokens,
    ids,
    gates,
    up,
    down,
    attended,
    combined,
    query_v,
    cache_v,
    up_v,
    down_v,
    rows_v,
    picked_v,
    gate_v,
    gathered_v,
    part_v,
    part_in,
    own_part,
    inner_v,
    inner_in,
    far_v,
    far_in,
    own_f,
    near_f,
    near_v,
    near_in,
    back_v,
    back_in,
    comb_v,
    comb_in,
    comb2a_in,
    comb2b_in,
    zsum,
    zsend,
    zsend_in,
    att_v,
    att_s,
    att_v_in,
    att_s_in,
    load_sem,
    send_sem,
    recv_sem,
):
    ctx, exp = lax.axis_index("ctx"), lax.axis_index("exp")
    x, core = ctx // 2, ctx % 2
    z, y = exp // NY, exp % NY
    sent = []

    def along_x(step):
        return (2 * ((x + step + NX) % NX) + core, exp)

    def along_y(step):
        return (ctx, NY * z + (y + step) % NY)

    def along_z(step):
        return (ctx, NY * ((z + step + NZ) % NZ) + y)

    sibling = (2 * x + 1 - core, exp)

    def send(src, dst, device):
        copy = pltpu.make_async_remote_copy(
            src_ref=src,
            dst_ref=dst,
            send_sem=send_sem.at[len(sent)],
            recv_sem=recv_sem.at[len(sent)],
            device_id=device,
            device_id_type=MESH,
        )
        copy.start()
        sent.append(copy)
        return copy

    loads = []

    def load(src, dst):
        copy = pltpu.make_async_copy(src, dst, load_sem.at[len(loads)])
        copy.start()
        loads.append(copy)
        return copy

    token_load = load(
        tokens.at[:, pl.ds(pl.multiple_of(ctx * WIDTH, 128), WIDTH)],
        rows_v.at[0, pl.ds(0, ROWS), pl.ds(0, WIDTH)],
    )

    partners = [along_z(d) for d in (4, -4, 8, 1, -1, 2, -2)]
    partners += [along_y(d) for d in (1, 2, 3)]
    partners += [((ctx + d) % 8, exp) for d in range(1, 8)]
    barrier = pltpu.get_barrier_semaphore()
    for partner in partners:
        pl.semaphore_signal(barrier, inc=1, device_id=partner, device_id_type=MESH)

    query_load = load(queries.at[0], query_v)
    cache_load = load(cache.at[0], cache_v)

    def up_rows(step, which):
        piece = 2 * ((x + step + NX) % NX) + (1 - core if which else core)
        return up.at[0, pl.ds(pl.multiple_of(piece * WIDTH, 128), WIDTH), :]

    def up_place(which, source):
        return up_v.at[which, :, pl.ds(source * UNITS, UNITS)]

    weight_loads = [load(up_rows(0, which), up_place(which, 0)) for which in (0, 1)]
    for r in range(NX):
        piece = pl.multiple_of((2 * ((x + r) % NX) + core) * WIDTH, 128)
        weight_loads.append(
            load(down.at[0, :, pl.ds(piece, WIDTH)], down_v.at[r, pl.ds(0, UNITS), :])
        )

    scores = gates[...]
    values = (scores / jnp.sum(scores, axis=0, keepdims=True) * ROUTE_SCALE).astype(BF16)
    values = values.astype(F32)
    chosen = ids[...]
    expert = lax.broadcasted_iota(jnp.int32, (TABLE, ROWS), 0)
    table = jnp.zeros((TABLE, ROWS), F32)
    for k in range(chosen.shape[0]):
        table = table + jnp.where(chosen[k : k + 1, :] == expert, values[k : k + 1, :], 0.0)
    unit_row = lax.broadcasted_iota(jnp.int32, (TABLE, TABLE), 0)
    unit_lane = lax.broadcasted_iota(jnp.int32, (TABLE, TABLE), 1)
    unit = jnp.where(unit_row == unit_lane, 1.0, 0.0).astype(BF16)
    rows_v[0, 0:ROWS, WIDTH:] = tn(table.astype(BF16), unit).astype(BF16)
    pl.semaphore_wait(barrier, len(partners))

    up_copies = []
    for step in (2, 1, -1):
        for which in (0, 1):
            up_copies.append(
                send(up_rows(step, which), up_place(which, (NX - step) % NX), along_x(step))
            )
    down_copies = []
    for r in range(NX):
        piece = pl.multiple_of((2 * ((x + r) % NX) + 1 - core) * WIDTH, 128)
        down_copies.append(
            send(
                down.at[0, :, pl.ds(piece, WIDTH)],
                down_v.at[r, pl.ds(UNITS, UNITS), :],
                sibling,
            )
        )

    def block(c, i):
        return rows_v.at[c, pl.ds(i % 4 * ROWS, ROWS), :]

    arrivals = {1: [], 2: [], 3: []}

    def forward(i):
        arrivals[1].append(send(block(0, i), block(1, i), along_z(-1)))
        arrivals[3].append(send(block(0, i), block(3, i - 1), along_z(1)))
        if i in (0, 3):
            arrivals[2].append(send(block(0, i), block(2, i - 1), along_z(2)))
        if i in (0, 1):
            arrivals[2].append(send(block(0, i), block(2, i), along_z(-2)))

    token_load.wait()
    from_low = send(block(0, 0), block(0, 3), along_z(4))
    from_high = send(block(0, 0), block(0, 1), along_z(-4))
    from_far = send(block(0, 0), block(0, 2), along_z(8))
    forward(0)

    def attend(t):
        score = tn(query_v[t], cache_v[...]) * SCALE
        position = ctx * KEYS + lax.broadcasted_iota(jnp.int32, (HEADS, KEYS), 1)
        live = position < lengths[0] - (1 - t)
        top = jnp.max(jnp.where(live, score, NEGATIVE), axis=1, keepdims=True)
        weight = jnp.where(live, jnp.exp(score - top), 0.0)
        total = jnp.sum(weight, axis=1, keepdims=True)
        value = nt(weight.astype(BF16), cache_v[0:LATENT, :])
        att_v[t] = value.astype(BF16)
        half = lax.broadcasted_iota(jnp.int32, (HEADS, 128), 1) < 64
        att_s[t] = jnp.where(half, top, total)

    query_load.wait()
    cache_load.wait()
    attend(0)
    from_low.wait_recv()
    forward(3)
    from_high.wait_recv()
    forward(1)
    from_far.wait_recv()
    forward(2)

    heads_copies = []

    def attend_send():
        for d in range(1, 8):
            other = (ctx + d) % 8
            heads = pl.ds(pl.multiple_of(other * OWN_HEADS, OWN_HEADS), OWN_HEADS)
            heads_copies.append(send(att_v.at[:, heads, :], att_v_in.at[d - 1], (other, exp)))
            heads_copies.append(send(att_s.at[:, heads, :], att_s_in.at[d - 1], (other, exp)))

    def attend_join():
        for copy in heads_copies:
            copy.wait_recv()
        heads = pl.ds(pl.multiple_of(ctx * OWN_HEADS, OWN_HEADS), OWN_HEADS)
        for t in range(2):
            stats = [att_s[t, heads, :]] + [att_s_in[d, t] for d in range(7)]
            parts = [att_v[t, heads, :]] + [att_v_in[d, t] for d in range(7)]
            top = functools.reduce(jnp.maximum, [s[:, 0:1] for s in stats])
            factors = [jnp.exp(s[:, 0:1] - top) for s in stats]
            total = sum(s[:, 64:65] * f for s, f in zip(stats, factors))
            accum = sum(p.astype(F32) * f for p, f in zip(parts, factors))
            attended[0, t] = (accum / total).astype(BF16)

    slot = lax.broadcasted_iota(jnp.int32, (SLOTS, SLOTS), 1)
    row = lax.broadcasted_iota(jnp.int32, (SLOTS, SLOTS), 0)
    same_block = (row // ROWS) == (slot % ROWS) // CAP
    slot_rank = (slot % CAP).astype(F32)
    earlier = jnp.where((row // ROWS == slot // ROWS) & (slot < row), 1.0, 0.0).astype(BF16)
    expert_lane = lax.broadcasted_iota(jnp.int32, (TABLE, SLOTS), 0)
    expert_slot = lax.broadcasted_iota(jnp.int32, (TABLE, SLOTS), 1)
    spread = jnp.where(
        expert_lane == NY * z + (y + expert_slot // ROWS) % NY, 1.0, 0.0
    ).astype(BF16)

    y_copies, pair_copies, part_copies, inner_copies = {}, {}, {}, {}
    far_copies, near_copies, back_copies, comb_copies = {}, {}, {}, {}

    def select(c):
        if c:
            for copy in arrivals[c]:
                copy.wait_recv()
        gate = rows_v[c, :, WIDTH:]
        named = jnp.where(gate.astype(F32) > 0, 1.0, 0.0).astype(BF16)
        rank = nn(earlier, named).astype(BF16)
        here = nn(named, spread)
        rank_here = nn(rank, spread)
        gate_here = nn(gate, spread)
        hit = (here > 0.5) & (rank_here == slot_rank) & same_block
        gate_v[c] = jnp.where(hit, gate_here, 0.0).astype(BF16)
        picked = tn(jnp.where(hit, 1.0, 0.0).astype(BF16), rows_v[c, :, 0:WIDTH]).astype(BF16)
        picked_v[c] = picked
        first = BACK.index(c) * SLOTS
        gathered_v[0, first : first + ROWS, :] = picked[0:ROWS]
        y_copies[c] = [
            send(
                picked_v.at[c, pl.ds(d * ROWS, ROWS), :],
                gathered_v.at[0, pl.ds(first + (NY - d) * ROWS, ROWS), :],
                along_y(d),
            )
            for d in (1, 2, 3)
        ]

    def pair(c):
        for copy in y_copies[c]:
            copy.wait_recv()
        rows = pl.ds(BACK.index(c) * SLOTS, SLOTS)
        pair_copies[c] = send(gathered_v.at[0, rows, :], gathered_v.at[1, rows, :], sibling)

    def rows_of(b):
        return pl.ds(b * 2 * SLOTS, 2 * SLOTS)

    def inner_part(b):
        if b == 0:
            for copy in weight_loads:
                copy.wait()
            for copy in up_copies:
                copy.wait_recv()
        for c in BACK[2 * b : 2 * b + 2]:
            pair_copies[c].wait_recv()
        part = nn(gathered_v[0, rows_of(b), :], up_v[0])
        part = part + nn(gathered_v[1, rows_of(b), :], up_v[1])
        own_part[b] = part[:, 0:UNITS]
        part_copies[b] = []
        for r in (2, 1, 3):
            part_v[b, r - 1] = part[:, r * UNITS : (r + 1) * UNITS].astype(BF16)
            part_copies[b].append(send(part_v.at[b, r - 1], part_in.at[b, r - 1], along_x(r)))

    def inner_sum(b):
        for copy in part_copies[b]:
            copy.wait_recv()
        total = own_part[b] + part_in[b, 0].astype(F32)
        total = total + part_in[b, 1].astype(F32) + part_in[b, 2].astype(F32)
        inner_v[b] = (total / (1.0 + jnp.exp(-total))).astype(BF16)
        inner_copies[b] = send(inner_v.at[b], inner_in.at[b], sibling)

    def outer_part(b):
        if b == 0:
            for copy in down_copies:
                copy.wait_recv()
        inner_copies[b].wait_recv()
        inner = jnp.concatenate([inner_v[b], inner_in[b]], axis=1)
        far = nn(inner, down_v[2]).astype(BF16)
        for i, c in enumerate(BACK[2 * b : 2 * b + 2]):
            far_v[c] = far[i * SLOTS : (i + 1) * SLOTS]
            low, high = pl.ds(0, SPLITS[c]), pl.ds(SPLITS[c], WIDTH - SPLITS[c])
            far_copies[c] = (
                send(far_v.at[c, :, low], far_in.at[c, :, low], along_x(1)),
                send(far_v.at[c, :, high], far_in.at[c, :, high], along_x(-1)),
            )
        near_f[b, 0] = nn(inner, down_v[1])
        near_f[b, 1] = nn(inner, down_v[3])
        own_f[b] = nn(inner, down_v[0])

    def half_of(c):
        b, i = divmod(BACK.index(c), 2)
        return b, pl.ds(i * SLOTS, SLOTS)

    def join_far(c):
        split = SPLITS[c]
        b, rows = half_of(c)
        up_near, down_near = near_f[b, 0, rows, :], near_f[b, 1, rows, :]
        for copy in far_copies[c]:
            copy.wait_recv()
        far_up, far_down = far_in[c, :, 0:split].astype(F32), far_in[c, :, split:].astype(F32)
        near_v[c, 0, :, 0:split] = (up_near[:, 0:split] + far_up).astype(BF16)
        near_v[c, 0, :, split:] = up_near[:, split:].astype(BF16)
        near_v[c, 1, :, 0:split] = down_near[:, 0:split].astype(BF16)
        near_v[c, 1, :, split:] = (down_near[:, split:] + far_down).astype(BF16)
        near_copies[c] = [
            [
                send(near_v.at[c, i, :, pl.ds(*part)], near_in.at[c, i, :, pl.ds(*part)], along_x(d))
                for i, d in ((0, 1), (1, -1))
            ]
            for part in COLUMNS[c]
        ]
        back_copies[c] = []

    def join_near(c, p=0):
        for copy in near_copies[c][p]:
            copy.wait_recv()
        b, rows = half_of(c)
        start, count = COLUMNS[c][p]
        part = pl.ds(start, count)
        total = own_f[b, rows, part] + near_in[c, 0, :, part].astype(F32)
        total = (total + near_in[c, 1, :, part].astype(F32)).astype(BF16)
        back_v[c, :, part] = total
        back_in[c, 0:ROWS, part] = total[0:ROWS]
        back_copies[c].append(
            [
                send(
                    back_v.at[c, pl.ds(d * ROWS, ROWS), part],
                    back_in.at[c, pl.ds((NY - d) * ROWS, ROWS), part],
                    along_y(d),
                )
                for d in (2, 1, 3)
            ]
        )

    def combine(c):
        for copy in back_copies[c][0]:
            copy.wait_recv()
        comb_v[c - 1] = nn(gate_v[c], back_in[c]).astype(BF16)
        half = 2 * ROWS
        if c == 1:
            comb_copies[1] = send(comb_v.at[0], comb_in.at[0], along_z(1))
        if c == 3:
            comb_copies[3] = send(comb_v.at[2], comb_in.at[1], along_z(-1))
        if c == 2:
            comb_copies[2] = (
                send(comb_v.at[1, pl.ds(0, half), :], comb2a_in, along_z(2)),
                send(comb_v.at[1, pl.ds(half, half), :], comb2b_in, along_z(-2)),
            )

    def from_neighbours():
        comb_copies[1].wait_recv()
        comb_copies[3].wait_recv()
        for copy in comb_copies[2]:
            copy.wait_recv()
        for i in range(4):
            j = (i + 3) % 4
            total = comb_in[0, i * ROWS : (i + 1) * ROWS, :].astype(F32)
            total = total + comb_in[1, j * ROWS : (j + 1) * ROWS, :].astype(F32)
            if i == 0:
                total = total + comb2a_in[0:ROWS, :].astype(F32) + comb2b_in[ROWS:, :].astype(F32)
            if i == 1:
                total = total + comb2a_in[ROWS:, :].astype(F32)
            if i == 3:
                total = total + comb2b_in[0:ROWS, :].astype(F32)
            zsum[i * ROWS : (i + 1) * ROWS, :] = total

    last_copies = []

    def join_z(p):
        for copy in back_copies[0][p]:
            copy.wait_recv()
        part = pl.ds(*COLUMNS[0][p])
        total = zsum[:, part] + nn(gate_v[0], back_in[0, :, part])
        zsum[0:ROWS, part] = total[0:ROWS]
        for i in (2, 1, 3):
            zsend[i - 1, :, part] = total[i * ROWS : (i + 1) * ROWS].astype(BF16)
            last_copies.append(
                send(zsend.at[i - 1, :, part], zsend_in.at[i - 1, :, part], along_z(4 * i))
            )

    select(0)
    attend(1)
    select(1)
    select(3)
    pair(0)
    select(2)
    pair(1)
    pair(3)
    pair(2)
    inner_part(0)
    inner_part(1)
    inner_sum(0)
    inner_sum(1)
    outer_part(0)
    outer_part(1)
    join_far(1)
    join_far(3)
    join_near(1)
    join_far(2)
    join_near(3)
    join_far(0)
    combine(1)
    join_near(2)
    combine(3)
    join_near(0, 0)
    combine(2)
    join_near(0, 1)
    attend_send()
    from_neighbours()
    join_z(0)
    join_z(1)
    attend_join()
    for copy in last_copies:
        copy.wait_recv()
    total = zsum[0:ROWS, :] + zsend_in[0].astype(F32)
    total = total + zsend_in[1].astype(F32) + zsend_in[2].astype(F32)
    combined[...] = total.astype(BF16)

    for copy in sent:
        copy.wait_send()
    assert len(sent) == n_send, len(sent)


N_SEND = 106
VMEM_LIMIT = 53 * 2**20 + 12 * 2**16


def shards(queries, cache, lengths, tokens, ids, gates, up, down):
    vmem = pl.BlockSpec(memory_space=pltpu.VMEM)
    hbm = pl.BlockSpec(memory_space=pl.ANY)
    smem = pl.BlockSpec(memory_space=pltpu.SMEM)
    n_classes = len(CLASSES)

    def buf(*shape, dtype=BF16):
        return pltpu.VMEM(shape, dtype)

    return pl.pallas_call(
        functools.partial(kernel, N_SEND),
        out_shape=(
            jax.ShapeDtypeStruct((1, 2, OWN_HEADS, LATENT), BF16),
            jax.ShapeDtypeStruct((ROWS, WIDTH), BF16),
        ),
        in_specs=[hbm, hbm, smem, hbm, vmem, vmem, hbm, hbm],
        out_specs=(vmem, vmem),
        scratch_shapes=[
            buf(2, 576, HEADS),
            buf(576, KEYS),
            buf(2, WIDTH, NX * UNITS),
            buf(NX, 256, WIDTH),
            buf(n_classes, SLOTS, WIDTH + TABLE),
            buf(n_classes, SLOTS, WIDTH),
            buf(n_classes, SLOTS, SLOTS),
            buf(2, n_classes * SLOTS, WIDTH),
            buf(2, 3, 2 * SLOTS, UNITS),
            buf(2, 3, 2 * SLOTS, UNITS),
            buf(2, 2 * SLOTS, UNITS, dtype=F32),
            buf(2, 2 * SLOTS, UNITS),
            buf(2, 2 * SLOTS, UNITS),
            buf(n_classes, SLOTS, WIDTH),
            buf(n_classes, SLOTS, WIDTH),
            buf(2, 2 * SLOTS, WIDTH, dtype=F32),
            buf(2, 2, 2 * SLOTS, WIDTH, dtype=F32),
            buf(n_classes, 2, SLOTS, WIDTH),
            buf(n_classes, 2, SLOTS, WIDTH),
            buf(n_classes, SLOTS, WIDTH),
            buf(n_classes, SLOTS, WIDTH),
            buf(3, SLOTS, WIDTH),
            buf(2, SLOTS, WIDTH),
            buf(2 * ROWS, WIDTH),
            buf(2 * ROWS, WIDTH),
            buf(SLOTS, WIDTH, dtype=F32),
            buf(3, ROWS, WIDTH),
            buf(3, ROWS, WIDTH),
            buf(2, HEADS, LATENT),
            buf(2, HEADS, 128, dtype=F32),
            buf(7, 2, OWN_HEADS, LATENT),
            buf(7, 2, OWN_HEADS, 128, dtype=F32),
            pltpu.SemaphoreType.DMA((9,)),
            pltpu.SemaphoreType.DMA((N_SEND,)),
            pltpu.SemaphoreType.DMA((N_SEND,)),
        ],
        compiler_params=pltpu.CompilerParams(
            collective_id=0, has_side_effects=True, vmem_limit_bytes=VMEM_LIMIT
        ),
    )(queries, cache, lengths, tokens, ids.T, gates.T, up, down)


def solution(mesh):
    in_specs = (
        P("exp", None, None, None),
        P("exp", None, "ctx"),
        P("exp"),
        P("exp", None),
        P("exp", None),
        P("exp", None),
        P("exp", None, "ctx"),
        P("exp", "ctx", None),
    )
    out_specs = (P("exp", None, "ctx", None), P("exp", "ctx"))
    return jax.shard_map(shards, mesh=mesh, in_specs=in_specs, out_specs=out_specs, check_vma=False)
```

```python
import functools

import jax
import jax.numpy as jnp
from jax import lax
from jax.experimental import pallas as pl
from jax.experimental.pallas import tpu as pltpu
from jax.sharding import PartitionSpec as P

MESH = pl.DeviceIdType.MESH
BF16, F32 = jnp.bfloat16, jnp.float32

SCALE = 192.0 ** (-0.5)
NEGATIVE = -1e30
ROUTE_SCALE = 2.5

NX, NY, NZ = 4, 4, 16
ROWS = 16
CAP = 4
WIDTH = 896
TABLE = 128
LATENT = 512
KEYS = 512
HEADS = 128
OWN_HEADS = 16
CLASSES = (0, 2, 1, 3)
BACK = (2, 1, 3, 0)
SPLITS = {1: 384, 3: 512, 2: 384, 0: 512}
COLUMNS = {1: ((0, 896),), 3: ((0, 896),), 2: ((0, 896),), 0: ((0, 512), (512, 384))}
UNITS = 128
SLOTS = 4 * ROWS


def nt(a, b):
    return lax.dot_general(a, b, (((1,), (1,)), ((), ())), preferred_element_type=F32)


def tn(a, b):
    return lax.dot_general(a, b, (((0,), (0,)), ((), ())), preferred_element_type=F32)


def nn(a, b):
    return jnp.dot(a, b, preferred_element_type=F32)


def kernel(
    n_send,
    queries,
    cache,
    lengths,
    tokens,
    ids,
    gates,
    up,
    down,
    attended,
    combined,
    query_v,
    cache_v,
    up_v,
    down_v,
    rows_v,
    picked_v,
    gate_v,
    gathered_v,
    part_v,
    part_in,
    own_part,
    inner_v,
    inner_in,
    far_v,
    far_in,
    own_f,
    near_f,
    near_v,
    near_in,
    back_v,
    back_in,
    comb_v,
    comb_in,
    comb2a_in,
    comb2b_in,
    zsum,
    zsend,
    zsend_in,
    att_v,
    att_s,
    att_v_in,
    att_s_in,
    load_sem,
    send_sem,
    recv_sem,
):
    ctx, exp = lax.axis_index("ctx"), lax.axis_index("exp")
    x, core = ctx // 2, ctx % 2
    z, y = exp // NY, exp % NY
    sent = []

    def along_x(step):
        return (2 * ((x + step + NX) % NX) + core, exp)

    def along_y(step):
        return (ctx, NY * z + (y + step) % NY)

    def along_z(step):
        return (ctx, NY * ((z + step + NZ) % NZ) + y)

    sibling = (2 * x + 1 - core, exp)

    def send(src, dst, device):
        copy = pltpu.make_async_remote_copy(
            src_ref=src,
            dst_ref=dst,
            send_sem=send_sem.at[len(sent)],
            recv_sem=recv_sem.at[len(sent)],
            device_id=device,
            device_id_type=MESH,
        )
        copy.start()
        sent.append(copy)
        return copy

    loads = []

    def load(src, dst):
        copy = pltpu.make_async_copy(src, dst, load_sem.at[len(loads)])
        copy.start()
        loads.append(copy)
        return copy

    token_load = load(
        tokens.at[:, pl.ds(pl.multiple_of(ctx * WIDTH, 128), WIDTH)],
        rows_v.at[0, pl.ds(0, ROWS), pl.ds(0, WIDTH)],
    )

    partners = [along_z(d) for d in (4, -4, 8, 1, -1, 2, -2)]
    partners += [along_y(d) for d in (1, 2, 3)]
    partners += [((ctx + d) % 8, exp) for d in range(1, 8)]
    barrier = pltpu.get_barrier_semaphore()
    for partner in partners:
        pl.semaphore_signal(barrier, inc=1, device_id=partner, device_id_type=MESH)

    query_load = load(queries.at[0], query_v)
    cache_load = load(cache.at[0], cache_v)

    def up_rows(step, which):
        piece = 2 * ((x + step + NX) % NX) + (1 - core if which else core)
        return up.at[0, pl.ds(pl.multiple_of(piece * WIDTH, 128), WIDTH), :]

    def up_place(which, source):
        return up_v.at[which, source]

    weight_loads = [load(up_rows(0, which), up_place(which, 0)) for which in (0, 1)]
    for r in range(NX):
        piece = pl.multiple_of((2 * ((x + r) % NX) + core) * WIDTH, 128)
        weight_loads.append(
            load(down.at[0, :, pl.ds(piece, WIDTH)], down_v.at[r, pl.ds(0, UNITS), :])
        )

    scores = gates[...]
    values = (scores / jnp.sum(scores, axis=0, keepdims=True) * ROUTE_SCALE).astype(BF16)
    values = values.astype(F32)
    chosen = ids[...]
    expert = lax.broadcasted_iota(jnp.int32, (TABLE, ROWS), 0)
    table = jnp.zeros((TABLE, ROWS), F32)
    for k in range(chosen.shape[0]):
        table = table + jnp.where(chosen[k : k + 1, :] == expert, values[k : k + 1, :], 0.0)
    unit_row = lax.broadcasted_iota(jnp.int32, (TABLE, TABLE), 0)
    unit_lane = lax.broadcasted_iota(jnp.int32, (TABLE, TABLE), 1)
    unit = jnp.where(unit_row == unit_lane, 1.0, 0.0).astype(BF16)
    rows_v[0, 0:ROWS, WIDTH:] = tn(table.astype(BF16), unit).astype(BF16)
    pl.semaphore_wait(barrier, len(partners))

    up_copies = []
    for step in (2, 1, -1):
        for which in (0, 1):
            up_copies.append(
                send(up_rows(step, which), up_place(which, (NX - step) % NX), along_x(step))
            )
    down_copies = []
    for r in range(NX):
        piece = pl.multiple_of((2 * ((x + r) % NX) + 1 - core) * WIDTH, 128)
        down_copies.append(
            send(
                down.at[0, :, pl.ds(piece, WIDTH)],
                down_v.at[r, pl.ds(UNITS, UNITS), :],
                sibling,
            )
        )

    def block(c, i):
        return rows_v.at[c, pl.ds(i % 4 * ROWS, ROWS), :]

    arrivals = {1: [], 2: [], 3: []}

    def forward(i):
        arrivals[1].append(send(block(0, i), block(1, i), along_z(-1)))
        arrivals[3].append(send(block(0, i), block(3, i - 1), along_z(1)))
        if i in (0, 3):
            arrivals[2].append(send(block(0, i), block(2, i - 1), along_z(2)))
        if i in (0, 1):
            arrivals[2].append(send(block(0, i), block(2, i), along_z(-2)))

    token_load.wait()
    from_low = send(block(0, 0), block(0, 3), along_z(4))
    from_high = send(block(0, 0), block(0, 1), along_z(-4))
    from_far = send(block(0, 0), block(0, 2), along_z(8))
    forward(0)

    def attend(t):
        score = tn(query_v[t], cache_v[...]) * SCALE
        position = ctx * KEYS + lax.broadcasted_iota(jnp.int32, (HEADS, KEYS), 1)
        live = position < lengths[0] - (1 - t)
        top = jnp.max(jnp.where(live, score, NEGATIVE), axis=1, keepdims=True)
        weight = jnp.where(live, jnp.exp(score - top), 0.0)
        total = jnp.sum(weight, axis=1, keepdims=True)
        value = nt(weight.astype(BF16), cache_v[0:LATENT, :])
        att_v[t] = value.astype(BF16)
        half = lax.broadcasted_iota(jnp.int32, (HEADS, 128), 1) < 64
        att_s[t] = jnp.where(half, top, total)

    query_load.wait()
    cache_load.wait()
    attend(0)
    from_low.wait_recv()
    forward(3)
    from_high.wait_recv()
    forward(1)
    from_far.wait_recv()
    forward(2)

    heads_copies = []

    def attend_send():
        for d in range(1, 8):
            other = (ctx + d) % 8
            heads = pl.ds(pl.multiple_of(other * OWN_HEADS, OWN_HEADS), OWN_HEADS)
            heads_copies.append(send(att_v.at[:, heads, :], att_v_in.at[d - 1], (other, exp)))
            heads_copies.append(send(att_s.at[:, heads, :], att_s_in.at[d - 1], (other, exp)))

    def attend_join():
        for copy in heads_copies:
            copy.wait_recv()
        heads = pl.ds(pl.multiple_of(ctx * OWN_HEADS, OWN_HEADS), OWN_HEADS)
        for t in range(2):
            stats = [att_s[t, heads, :]] + [att_s_in[d, t] for d in range(7)]
            parts = [att_v[t, heads, :]] + [att_v_in[d, t] for d in range(7)]
            top = functools.reduce(jnp.maximum, [s[:, 0:1] for s in stats])
            factors = [jnp.exp(s[:, 0:1] - top) for s in stats]
            total = sum(s[:, 64:65] * f for s, f in zip(stats, factors))
            accum = sum(p.astype(F32) * f for p, f in zip(parts, factors))
            attended[0, t] = (accum / total).astype(BF16)

    slot = lax.broadcasted_iota(jnp.int32, (SLOTS, SLOTS), 1)
    row = lax.broadcasted_iota(jnp.int32, (SLOTS, SLOTS), 0)
    same_block = (row // ROWS) == (slot % ROWS) // CAP
    slot_rank = (slot % CAP).astype(F32)
    earlier = jnp.where((row // ROWS == slot // ROWS) & (slot < row), 1.0, 0.0).astype(BF16)
    expert_lane = lax.broadcasted_iota(jnp.int32, (TABLE, SLOTS), 0)
    expert_slot = lax.broadcasted_iota(jnp.int32, (TABLE, SLOTS), 1)
    spread = jnp.where(
        expert_lane == NY * z + (y + expert_slot // ROWS) % NY, 1.0, 0.0
    ).astype(BF16)

    y_copies, pair_copies, part_copies, inner_copies = {}, {}, {}, {}
    far_copies, near_copies, back_copies, comb_copies = {}, {}, {}, {}

    def select(c):
        if c:
            for copy in arrivals[c]:
                copy.wait_recv()
        gate = rows_v[c, :, WIDTH:]
        named = jnp.where(gate.astype(F32) > 0, 1.0, 0.0).astype(BF16)
        rank = nn(earlier, named).astype(BF16)
        here = nn(named, spread)
        rank_here = nn(rank, spread)
        gate_here = nn(gate, spread)
        hit = (here > 0.5) & (rank_here == slot_rank) & same_block
        gate_v[c] = jnp.where(hit, gate_here, 0.0).astype(BF16)
        picked = tn(jnp.where(hit, 1.0, 0.0).astype(BF16), rows_v[c, :, 0:WIDTH]).astype(BF16)
        picked_v[c] = picked
        first = BACK.index(c) * SLOTS
        gathered_v[0, first : first + ROWS, :] = picked[0:ROWS]
        y_copies[c] = [
            send(
                picked_v.at[c, pl.ds(d * ROWS, ROWS), :],
                gathered_v.at[0, pl.ds(first + (NY - d) * ROWS, ROWS), :],
                along_y(d),
            )
            for d in (1, 2, 3)
        ]

    def pair(c):
        for copy in y_copies[c]:
            copy.wait_recv()
        rows = pl.ds(BACK.index(c) * SLOTS, SLOTS)
        pair_copies[c] = send(gathered_v.at[0, rows, :], gathered_v.at[1, rows, :], sibling)

    def rows_of(b):
        return pl.ds(b * 2 * SLOTS, 2 * SLOTS)

    def inner_part(b):
        if b == 0:
            for copy in weight_loads:
                copy.wait()
            for copy in up_copies:
                copy.wait_recv()
        for c in BACK[2 * b : 2 * b + 2]:
            pair_copies[c].wait_recv()
        ups = [jnp.concatenate([up_v[w, r] for r in range(NX)], axis=1) for w in (0, 1)]
        part = nn(gathered_v[0, rows_of(b), :], ups[0])
        part = part + nn(gathered_v[1, rows_of(b), :], ups[1])
        own_part[b] = part[:, 0:UNITS]
        part_copies[b] = []
        for r in (2, 1, 3):
            part_v[b, r - 1] = part[:, r * UNITS : (r + 1) * UNITS].astype(BF16)
            part_copies[b].append(send(part_v.at[b, r - 1], part_in.at[b, r - 1], along_x(r)))

    def inner_sum(b):
        for copy in part_copies[b]:
            copy.wait_recv()
        total = own_part[b] + part_in[b, 0].astype(F32)
        total = total + part_in[b, 1].astype(F32) + part_in[b, 2].astype(F32)
        inner_v[b] = (total / (1.0 + jnp.exp(-total))).astype(BF16)
        inner_copies[b] = send(inner_v.at[b], inner_in.at[b], sibling)

    def outer(b, r):
        return nn(jnp.concatenate([inner_v[b], inner_in[b]], axis=1), down_v[r])

    def outer_far(b):
        if b == 0:
            for copy in down_copies:
                copy.wait_recv()
        inner_copies[b].wait_recv()
        far = outer(b, 2).astype(BF16)
        for i, c in enumerate(BACK[2 * b : 2 * b + 2]):
            far_v[c] = far[i * SLOTS : (i + 1) * SLOTS]
            low, high = pl.ds(0, SPLITS[c]), pl.ds(SPLITS[c], WIDTH - SPLITS[c])
            far_copies[c] = (
                send(far_v.at[c, :, low], far_in.at[c, :, low], along_x(1)),
                send(far_v.at[c, :, high], far_in.at[c, :, high], along_x(-1)),
            )

    def outer_near(b):
        near_f[b, 0] = outer(b, 1)
        near_f[b, 1] = outer(b, 3)
        own_f[b] = outer(b, 0)

    def half_of(c):
        b, i = divmod(BACK.index(c), 2)
        return b, pl.ds(i * SLOTS, SLOTS)

    def join_far(c):
        split = SPLITS[c]
        b, rows = half_of(c)
        up_near, down_near = near_f[b, 0, rows, :], near_f[b, 1, rows, :]
        for copy in far_copies[c]:
            copy.wait_recv()
        far_up, far_down = far_in[c, :, 0:split].astype(F32), far_in[c, :, split:].astype(F32)
        near_v[c, 0, :, 0:split] = (up_near[:, 0:split] + far_up).astype(BF16)
        near_v[c, 0, :, split:] = up_near[:, split:].astype(BF16)
        near_v[c, 1, :, 0:split] = down_near[:, 0:split].astype(BF16)
        near_v[c, 1, :, split:] = (down_near[:, split:] + far_down).astype(BF16)
        near_copies[c] = [
            [
                send(near_v.at[c, i, :, pl.ds(*part)], near_in.at[c, i, :, pl.ds(*part)], along_x(d))
                for i, d in ((0, 1), (1, -1))
            ]
            for part in COLUMNS[c]
        ]
        back_copies[c] = []

    def join_near(c, p=0):
        for copy in near_copies[c][p]:
            copy.wait_recv()
        b, rows = half_of(c)
        start, count = COLUMNS[c][p]
        part = pl.ds(start, count)
        total = own_f[b, rows, part] + near_in[c, 0, :, part].astype(F32)
        total = (total + near_in[c, 1, :, part].astype(F32)).astype(BF16)
        back_v[c, :, part] = total
        back_in[c, 0:ROWS, part] = total[0:ROWS]
        back_copies[c].append(
            [
                send(
                    back_v.at[c, pl.ds(d * ROWS, ROWS), part],
                    back_in.at[c, pl.ds((NY - d) * ROWS, ROWS), part],
                    along_y(d),
                )
                for d in (2, 1, 3)
            ]
        )

    def combine(c):
        for copy in back_copies[c][0]:
            copy.wait_recv()
        comb_v[c - 1] = nn(gate_v[c], back_in[c]).astype(BF16)
        half = 2 * ROWS
        if c == 1:
            comb_copies[1] = send(comb_v.at[0], comb_in.at[0], along_z(1))
        if c == 3:
            comb_copies[3] = send(comb_v.at[2], comb_in.at[1], along_z(-1))
        if c == 2:
            comb_copies[2] = (
                send(comb_v.at[1, pl.ds(0, half), :], comb2a_in, along_z(2)),
                send(comb_v.at[1, pl.ds(half, half), :], comb2b_in, along_z(-2)),
            )

    def from_neighbours():
        comb_copies[1].wait_recv()
        comb_copies[3].wait_recv()
        for copy in comb_copies[2]:
            copy.wait_recv()
        for i in range(4):
            j = (i + 3) % 4
            total = comb_in[0, i * ROWS : (i + 1) * ROWS, :].astype(F32)
            total = total + comb_in[1, j * ROWS : (j + 1) * ROWS, :].astype(F32)
            if i == 0:
                total = total + comb2a_in[0:ROWS, :].astype(F32) + comb2b_in[ROWS:, :].astype(F32)
            if i == 1:
                total = total + comb2a_in[ROWS:, :].astype(F32)
            if i == 3:
                total = total + comb2b_in[0:ROWS, :].astype(F32)
            zsum[i * ROWS : (i + 1) * ROWS, :] = total

    last_copies = []

    def join_z(p):
        for copy in back_copies[0][p]:
            copy.wait_recv()
        part = pl.ds(*COLUMNS[0][p])
        total = zsum[:, part] + nn(gate_v[0], back_in[0, :, part])
        zsum[0:ROWS, part] = total[0:ROWS]
        for i in (2, 1, 3):
            zsend[i - 1, :, part] = total[i * ROWS : (i + 1) * ROWS].astype(BF16)
            last_copies.append(
                send(zsend.at[i - 1, :, part], zsend_in.at[i - 1, :, part], along_z(4 * i))
            )

    select(0)
    attend(1)
    select(2)
    select(1)
    pair(0)
    select(3)
    pair(2)
    pair(1)
    pair(3)
    inner_part(0)
    inner_part(1)
    inner_sum(0)
    outer_far(0)
    inner_sum(1)
    outer_near(0)
    outer_far(1)
    join_far(2)
    join_far(1)
    outer_near(1)
    join_near(2)
    join_far(3)
    join_near(1)
    join_far(0)
    combine(2)
    join_near(3)
    combine(1)
    join_near(0, 0)
    combine(3)
    join_near(0, 1)
    attend_send()
    from_neighbours()
    join_z(0)
    join_z(1)
    attend_join()
    for copy in last_copies:
        copy.wait_recv()
    total = zsum[0:ROWS, :] + zsend_in[0].astype(F32)
    total = total + zsend_in[1].astype(F32) + zsend_in[2].astype(F32)
    combined[...] = total.astype(BF16)

    for copy in sent:
        copy.wait_send()
    assert len(sent) == n_send, len(sent)


N_SEND = 106
VMEM_LIMIT = 53 * 2**20 + 12 * 2**16


def shards(queries, cache, lengths, tokens, ids, gates, up, down):
    vmem = pl.BlockSpec(memory_space=pltpu.VMEM)
    hbm = pl.BlockSpec(memory_space=pl.ANY)
    smem = pl.BlockSpec(memory_space=pltpu.SMEM)
    n_classes = len(CLASSES)

    def buf(*shape, dtype=BF16):
        return pltpu.VMEM(shape, dtype)

    return pl.pallas_call(
        functools.partial(kernel, N_SEND),
        out_shape=(
            jax.ShapeDtypeStruct((1, 2, OWN_HEADS, LATENT), BF16),
            jax.ShapeDtypeStruct((ROWS, WIDTH), BF16),
        ),
        in_specs=[hbm, hbm, smem, hbm, vmem, vmem, hbm, hbm],
        out_specs=(vmem, vmem),
        scratch_shapes=[
            buf(2, 576, HEADS),
            buf(576, KEYS),
            buf(2, NX, WIDTH, UNITS),
            buf(NX, 256, WIDTH),
            buf(n_classes, SLOTS, WIDTH + TABLE),
            buf(n_classes, SLOTS, WIDTH),
            buf(n_classes, SLOTS, SLOTS),
            buf(2, n_classes * SLOTS, WIDTH),
            buf(2, 3, 2 * SLOTS, UNITS),
            buf(2, 3, 2 * SLOTS, UNITS),
            buf(2, 2 * SLOTS, UNITS, dtype=F32),
            buf(2, 2 * SLOTS, UNITS),
            buf(2, 2 * SLOTS, UNITS),
            buf(n_classes, SLOTS, WIDTH),
            buf(n_classes, SLOTS, WIDTH),
            buf(2, 2 * SLOTS, WIDTH, dtype=F32),
            buf(2, 2, 2 * SLOTS, WIDTH, dtype=F32),
            buf(n_classes, 2, SLOTS, WIDTH),
            buf(n_classes, 2, SLOTS, WIDTH),
            buf(n_classes, SLOTS, WIDTH),
            buf(n_classes, SLOTS, WIDTH),
            buf(3, SLOTS, WIDTH),
            buf(2, SLOTS, WIDTH),
            buf(2 * ROWS, WIDTH),
            buf(2 * ROWS, WIDTH),
            buf(SLOTS, WIDTH, dtype=F32),
            buf(3, ROWS, WIDTH),
            buf(3, ROWS, WIDTH),
            buf(2, HEADS, LATENT),
            buf(2, HEADS, 128, dtype=F32),
            buf(7, 2, OWN_HEADS, LATENT),
            buf(7, 2, OWN_HEADS, 128, dtype=F32),
            pltpu.SemaphoreType.DMA((9,)),
            pltpu.SemaphoreType.DMA((N_SEND,)),
            pltpu.SemaphoreType.DMA((N_SEND,)),
        ],
        compiler_params=pltpu.CompilerParams(
            collective_id=0, has_side_effects=True, vmem_limit_bytes=VMEM_LIMIT
        ),
    )(queries, cache, lengths, tokens, ids.T, gates.T, up, down)


def solution(mesh):
    in_specs = (
        P("exp", None, None, None),
        P("exp", None, "ctx"),
        P("exp"),
        P("exp", None),
        P("exp", None),
        P("exp", None),
        P("exp", None, "ctx"),
        P("exp", "ctx", None),
    )
    out_specs = (P("exp", None, "ctx", None), P("exp", "ctx"))
    return jax.shard_map(shards, mesh=mesh, in_specs=in_specs, out_specs=out_specs, check_vma=False)
```

```python
import functools

import jax
import jax.numpy as jnp
from jax import lax
from jax.experimental import pallas as pl
from jax.experimental.pallas import tpu as pltpu
from jax.sharding import PartitionSpec as P

MESH = pl.DeviceIdType.MESH
BF16, F32 = jnp.bfloat16, jnp.float32

SCALE = 192.0 ** (-0.5)
NEGATIVE = -1e30
ROUTE_SCALE = 2.5

NX, NY, NZ = 4, 4, 16
ROWS = 16
CAP = 4
WIDTH = 896
TABLE = 128
LATENT = 512
KEYS = 512
HEADS = 128
OWN_HEADS = 16
CLASSES = (0, 2, 1, 3)
BACK = (2, 1, 3, 0)
SPLITS = {1: 384, 3: 512, 2: 384, 0: 512}
COLUMNS = {1: ((0, 896),), 3: ((0, 896),), 2: ((0, 896),), 0: ((0, 512), (512, 384))}
UNITS = 128
SLOTS = 4 * ROWS


def nt(a, b):
    return lax.dot_general(a, b, (((1,), (1,)), ((), ())), preferred_element_type=F32)


def tn(a, b):
    return lax.dot_general(a, b, (((0,), (0,)), ((), ())), preferred_element_type=F32)


def nn(a, b):
    return jnp.dot(a, b, preferred_element_type=F32)


def kernel(
    n_send,
    queries,
    cache,
    lengths,
    tokens,
    ids,
    gates,
    up,
    down,
    attended,
    combined,
    query_v,
    cache_v,
    up_v,
    down_v,
    rows_v,
    picked_v,
    gate_v,
    gathered_v,
    part_v,
    part_in,
    own_part,
    inner_v,
    inner_in,
    far_v,
    far_in,
    own_f,
    near_f,
    near_v,
    near_in,
    back_v,
    back_in,
    comb_v,
    comb_in,
    comb2a_in,
    comb2b_in,
    zsum,
    zsend,
    zsend_in,
    att_v,
    att_s,
    att_v_in,
    att_s_in,
    load_sem,
    send_sem,
    recv_sem,
):
    ctx, exp = lax.axis_index("ctx"), lax.axis_index("exp")
    x, core = ctx // 2, ctx % 2
    z, y = exp // NY, exp % NY
    sent = []

    def along_x(step):
        return (2 * ((x + step + NX) % NX) + core, exp)

    def along_y(step):
        return (ctx, NY * z + (y + step) % NY)

    def along_z(step):
        return (ctx, NY * ((z + step + NZ) % NZ) + y)

    sibling = (2 * x + 1 - core, exp)

    def send(src, dst, device):
        copy = pltpu.make_async_remote_copy(
            src_ref=src,
            dst_ref=dst,
            send_sem=send_sem.at[len(sent)],
            recv_sem=recv_sem.at[len(sent)],
            device_id=device,
            device_id_type=MESH,
        )
        copy.start()
        sent.append(copy)
        return copy

    loads = []

    def load(src, dst):
        copy = pltpu.make_async_copy(src, dst, load_sem.at[len(loads)])
        copy.start()
        loads.append(copy)
        return copy

    token_load = load(
        tokens.at[:, pl.ds(pl.multiple_of(ctx * WIDTH, 128), WIDTH)],
        rows_v.at[0, pl.ds(0, ROWS), pl.ds(0, WIDTH)],
    )

    partners = [along_z(d) for d in (4, -4, 8, 1, -1, 2, -2)]
    partners += [along_y(d) for d in (1, 2, 3)]
    partners += [((ctx + d) % 8, exp) for d in range(1, 8)]
    barrier = pltpu.get_barrier_semaphore()
    for partner in partners:
        pl.semaphore_signal(barrier, inc=1, device_id=partner, device_id_type=MESH)

    query_load = load(queries.at[0], query_v)
    cache_load = load(cache.at[0], cache_v)

    def up_rows(step, which):
        piece = 2 * ((x + step + NX) % NX) + (1 - core if which else core)
        return up.at[0, pl.ds(pl.multiple_of(piece * WIDTH, 128), WIDTH), :]

    def up_place(which, source):
        return up_v.at[which, source]

    weight_loads = [load(up_rows(0, which), up_place(which, 0)) for which in (0, 1)]
    for r in range(NX):
        piece = pl.multiple_of((2 * ((x + r) % NX) + core) * WIDTH, 128)
        weight_loads.append(
            load(down.at[0, :, pl.ds(piece, WIDTH)], down_v.at[r, pl.ds(0, UNITS), :])
        )

    scores = gates[...]
    values = (scores / jnp.sum(scores, axis=0, keepdims=True) * ROUTE_SCALE).astype(BF16)
    values = values.astype(F32)
    chosen = ids[...]
    expert = lax.broadcasted_iota(jnp.int32, (TABLE, ROWS), 0)
    table = jnp.zeros((TABLE, ROWS), F32)
    for k in range(chosen.shape[0]):
        table = table + jnp.where(chosen[k : k + 1, :] == expert, values[k : k + 1, :], 0.0)
    unit_row = lax.broadcasted_iota(jnp.int32, (TABLE, TABLE), 0)
    unit_lane = lax.broadcasted_iota(jnp.int32, (TABLE, TABLE), 1)
    unit = jnp.where(unit_row == unit_lane, 1.0, 0.0).astype(BF16)
    rows_v[0, 0:ROWS, WIDTH:] = tn(table.astype(BF16), unit).astype(BF16)
    pl.semaphore_wait(barrier, len(partners))

    up_copies = []
    for step in (2, 1, -1):
        for which in (0, 1):
            up_copies.append(
                send(up_rows(step, which), up_place(which, (NX - step) % NX), along_x(step))
            )
    down_copies = []
    for r in range(NX):
        piece = pl.multiple_of((2 * ((x + r) % NX) + 1 - core) * WIDTH, 128)
        down_copies.append(
            send(
                down.at[0, :, pl.ds(piece, WIDTH)],
                down_v.at[r, pl.ds(UNITS, UNITS), :],
                sibling,
            )
        )

    def block(c, i):
        return rows_v.at[c, pl.ds(i % 4 * ROWS, ROWS), :]

    arrivals = {1: [], 2: [], 3: []}

    def forward(i):
        arrivals[1].append(send(block(0, i), block(1, i), along_z(-1)))
        arrivals[3].append(send(block(0, i), block(3, i - 1), along_z(1)))
        if i in (0, 3):
            arrivals[2].append(send(block(0, i), block(2, i - 1), along_z(2)))
        if i in (0, 1):
            arrivals[2].append(send(block(0, i), block(2, i), along_z(-2)))

    token_load.wait()
    from_far = send(block(0, 0), block(0, 2), along_z(8))
    from_low = send(block(0, 0), block(0, 3), along_z(4))
    from_high = send(block(0, 0), block(0, 1), along_z(-4))
    forward(0)

    def attend(t):
        score = tn(query_v[t], cache_v[...]) * SCALE
        position = ctx * KEYS + lax.broadcasted_iota(jnp.int32, (HEADS, KEYS), 1)
        live = position < lengths[0] - (1 - t)
        top = jnp.max(jnp.where(live, score, NEGATIVE), axis=1, keepdims=True)
        weight = jnp.where(live, jnp.exp(score - top), 0.0)
        total = jnp.sum(weight, axis=1, keepdims=True)
        value = nt(weight.astype(BF16), cache_v[0:LATENT, :])
        att_v[t] = value.astype(BF16)
        half = lax.broadcasted_iota(jnp.int32, (HEADS, 128), 1) < 64
        att_s[t] = jnp.where(half, top, total)

    query_load.wait()
    cache_load.wait()
    attend(0)
    from_low.wait_recv()
    forward(3)
    from_high.wait_recv()
    forward(1)
    from_far.wait_recv()
    forward(2)

    heads_copies = []

    def attend_send():
        for d in range(1, 8):
            other = (ctx + d) % 8
            heads = pl.ds(pl.multiple_of(other * OWN_HEADS, OWN_HEADS), OWN_HEADS)
            heads_copies.append(send(att_v.at[:, heads, :], att_v_in.at[d - 1], (other, exp)))
            heads_copies.append(send(att_s.at[:, heads, :], att_s_in.at[d - 1], (other, exp)))

    def attend_join():
        for copy in heads_copies:
            copy.wait_recv()
        heads = pl.ds(pl.multiple_of(ctx * OWN_HEADS, OWN_HEADS), OWN_HEADS)
        for t in range(2):
            stats = [att_s[t, heads, :]] + [att_s_in[d, t] for d in range(7)]
            parts = [att_v[t, heads, :]] + [att_v_in[d, t] for d in range(7)]
            top = functools.reduce(jnp.maximum, [s[:, 0:1] for s in stats])
            factors = [jnp.exp(s[:, 0:1] - top) for s in stats]
            total = sum(s[:, 64:65] * f for s, f in zip(stats, factors))
            accum = sum(p.astype(F32) * f for p, f in zip(parts, factors))
            attended[0, t] = (accum / total).astype(BF16)

    slot = lax.broadcasted_iota(jnp.int32, (SLOTS, SLOTS), 1)
    row = lax.broadcasted_iota(jnp.int32, (SLOTS, SLOTS), 0)
    same_block = (row // ROWS) == (slot % ROWS) // CAP
    slot_rank = (slot % CAP).astype(F32)
    earlier = jnp.where((row // ROWS == slot // ROWS) & (slot < row), 1.0, 0.0).astype(BF16)
    expert_lane = lax.broadcasted_iota(jnp.int32, (TABLE, SLOTS), 0)
    expert_slot = lax.broadcasted_iota(jnp.int32, (TABLE, SLOTS), 1)
    spread = jnp.where(
        expert_lane == NY * z + (y + expert_slot // ROWS) % NY, 1.0, 0.0
    ).astype(BF16)

    y_copies, pair_copies, part_copies, inner_copies = {}, {}, {}, {}
    far_copies, near_copies, back_copies, comb_copies = {}, {}, {}, {}

    def select(c):
        if c:
            for copy in arrivals[c]:
                copy.wait_recv()
        gate = rows_v[c, :, WIDTH:]
        named = jnp.where(gate.astype(F32) > 0, 1.0, 0.0).astype(BF16)
        rank = nn(earlier, named).astype(BF16)
        here = nn(named, spread)
        rank_here = nn(rank, spread)
        gate_here = nn(gate, spread)
        hit = (here > 0.5) & (rank_here == slot_rank) & same_block
        gate_v[c] = jnp.where(hit, gate_here, 0.0).astype(BF16)
        picked = tn(jnp.where(hit, 1.0, 0.0).astype(BF16), rows_v[c, :, 0:WIDTH]).astype(BF16)
        picked_v[c] = picked
        first = BACK.index(c) * SLOTS
        gathered_v[0, first : first + ROWS, :] = picked[0:ROWS]
        y_copies[c] = [
            send(
                picked_v.at[c, pl.ds(d * ROWS, ROWS), :],
                gathered_v.at[0, pl.ds(first + (NY - d) * ROWS, ROWS), :],
                along_y(d),
            )
            for d in (1, 2, 3)
        ]

    def pair(c):
        for copy in y_copies[c]:
            copy.wait_recv()
        rows = pl.ds(BACK.index(c) * SLOTS, SLOTS)
        pair_copies[c] = send(gathered_v.at[0, rows, :], gathered_v.at[1, rows, :], sibling)

    def rows_of(b):
        return pl.ds(b * 2 * SLOTS, 2 * SLOTS)

    def inner_part(b):
        if b == 0:
            for copy in weight_loads:
                copy.wait()
            for copy in up_copies:
                copy.wait_recv()
        for c in BACK[2 * b : 2 * b + 2]:
            pair_copies[c].wait_recv()
        ups = [jnp.concatenate([up_v[w, r] for r in range(NX)], axis=1) for w in (0, 1)]
        part = nn(gathered_v[0, rows_of(b), :], ups[0])
        part = part + nn(gathered_v[1, rows_of(b), :], ups[1])
        own_part[b] = part[:, 0:UNITS]
        part_copies[b] = []
        for r in (2, 1, 3):
            part_v[b, r - 1] = part[:, r * UNITS : (r + 1) * UNITS].astype(BF16)
            part_copies[b].append(send(part_v.at[b, r - 1], part_in.at[b, r - 1], along_x(r)))

    def inner_sum(b):
        for copy in part_copies[b]:
            copy.wait_recv()
        total = own_part[b] + part_in[b, 0].astype(F32)
        total = total + part_in[b, 1].astype(F32) + part_in[b, 2].astype(F32)
        inner_v[b] = (total / (1.0 + jnp.exp(-total))).astype(BF16)
        inner_copies[b] = send(inner_v.at[b], inner_in.at[b], sibling)

    def outer(b, r):
        return nn(jnp.concatenate([inner_v[b], inner_in[b]], axis=1), down_v[r])

    def outer_far(b):
        if b == 0:
            for copy in down_copies:
                copy.wait_recv()
        inner_copies[b].wait_recv()
        far = outer(b, 2).astype(BF16)
        for i, c in enumerate(BACK[2 * b : 2 * b + 2]):
            far_v[c] = far[i * SLOTS : (i + 1) * SLOTS]
            low, high = pl.ds(0, SPLITS[c]), pl.ds(SPLITS[c], WIDTH - SPLITS[c])
            far_copies[c] = (
                send(far_v.at[c, :, low], far_in.at[c, :, low], along_x(1)),
                send(far_v.at[c, :, high], far_in.at[c, :, high], along_x(-1)),
            )

    def outer_near(b):
        near_f[b, 0] = outer(b, 1)
        near_f[b, 1] = outer(b, 3)
        own_f[b] = outer(b, 0)

    def half_of(c):
        b, i = divmod(BACK.index(c), 2)
        return b, pl.ds(i * SLOTS, SLOTS)

    def join_far(c):
        split = SPLITS[c]
        b, rows = half_of(c)
        up_near, down_near = near_f[b, 0, rows, :], near_f[b, 1, rows, :]
        for copy in far_copies[c]:
            copy.wait_recv()
        far_up, far_down = far_in[c, :, 0:split].astype(F32), far_in[c, :, split:].astype(F32)
        near_v[c, 0, :, 0:split] = (up_near[:, 0:split] + far_up).astype(BF16)
        near_v[c, 0, :, split:] = up_near[:, split:].astype(BF16)
        near_v[c, 1, :, 0:split] = down_near[:, 0:split].astype(BF16)
        near_v[c, 1, :, split:] = (down_near[:, split:] + far_down).astype(BF16)
        near_copies[c] = [
            [
                send(near_v.at[c, i, :, pl.ds(*part)], near_in.at[c, i, :, pl.ds(*part)], along_x(d))
                for i, d in ((0, 1), (1, -1))
            ]
            for part in COLUMNS[c]
        ]
        back_copies[c] = []

    def join_near(c, p=0):
        for copy in near_copies[c][p]:
            copy.wait_recv()
        b, rows = half_of(c)
        start, count = COLUMNS[c][p]
        part = pl.ds(start, count)
        total = own_f[b, rows, part] + near_in[c, 0, :, part].astype(F32)
        total = (total + near_in[c, 1, :, part].astype(F32)).astype(BF16)
        back_v[c, :, part] = total
        back_in[c, 0:ROWS, part] = total[0:ROWS]
        back_copies[c].append(
            [
                send(
                    back_v.at[c, pl.ds(d * ROWS, ROWS), part],
                    back_in.at[c, pl.ds((NY - d) * ROWS, ROWS), part],
                    along_y(d),
                )
                for d in (2, 1, 3)
            ]
        )

    def combine(c):
        for copy in back_copies[c][0]:
            copy.wait_recv()
        comb_v[c - 1] = nn(gate_v[c], back_in[c]).astype(BF16)
        half = 2 * ROWS
        if c == 1:
            comb_copies[1] = send(comb_v.at[0], comb_in.at[0], along_z(1))
        if c == 3:
            comb_copies[3] = send(comb_v.at[2], comb_in.at[1], along_z(-1))
        if c == 2:
            comb_copies[2] = (
                send(comb_v.at[1, pl.ds(0, half), :], comb2a_in, along_z(2)),
                send(comb_v.at[1, pl.ds(half, half), :], comb2b_in, along_z(-2)),
            )

    def from_neighbours():
        comb_copies[1].wait_recv()
        comb_copies[3].wait_recv()
        for copy in comb_copies[2]:
            copy.wait_recv()
        for i in range(4):
            j = (i + 3) % 4
            total = comb_in[0, i * ROWS : (i + 1) * ROWS, :].astype(F32)
            total = total + comb_in[1, j * ROWS : (j + 1) * ROWS, :].astype(F32)
            if i == 0:
                total = total + comb2a_in[0:ROWS, :].astype(F32) + comb2b_in[ROWS:, :].astype(F32)
            if i == 1:
                total = total + comb2a_in[ROWS:, :].astype(F32)
            if i == 3:
                total = total + comb2b_in[0:ROWS, :].astype(F32)
            zsum[i * ROWS : (i + 1) * ROWS, :] = total

    last_copies = []

    def join_z(p):
        for copy in back_copies[0][p]:
            copy.wait_recv()
        part = pl.ds(*COLUMNS[0][p])
        total = zsum[:, part] + nn(gate_v[0], back_in[0, :, part])
        zsum[0:ROWS, part] = total[0:ROWS]
        for i in (2, 1, 3):
            zsend[i - 1, :, part] = total[i * ROWS : (i + 1) * ROWS].astype(BF16)
            last_copies.append(
                send(zsend.at[i - 1, :, part], zsend_in.at[i - 1, :, part], along_z(4 * i))
            )

    select(0)
    attend(1)
    select(2)
    select(1)
    pair(0)
    select(3)
    pair(2)
    pair(1)
    pair(3)
    inner_part(0)
    inner_part(1)
    inner_sum(0)
    outer_far(0)
    inner_sum(1)
    outer_far(1)
    outer_near(0)
    join_far(2)
    join_far(1)
    outer_near(1)
    join_near(2)
    join_far(3)
    join_near(1)
    join_far(0)
    combine(2)
    join_near(3)
    combine(1)
    join_near(0, 0)
    combine(3)
    join_near(0, 1)
    attend_send()
    from_neighbours()
    join_z(0)
    join_z(1)
    attend_join()
    for copy in last_copies:
        copy.wait_recv()
    total = zsum[0:ROWS, :] + zsend_in[0].astype(F32)
    total = total + zsend_in[1].astype(F32) + zsend_in[2].astype(F32)
    combined[...] = total.astype(BF16)

    for copy in sent:
        copy.wait_send()
    assert len(sent) == n_send, len(sent)


N_SEND = 106
VMEM_LIMIT = 53 * 2**20 + 12 * 2**16


def shards(queries, cache, lengths, tokens, ids, gates, up, down):
    vmem = pl.BlockSpec(memory_space=pltpu.VMEM)
    hbm = pl.BlockSpec(memory_space=pl.ANY)
    smem = pl.BlockSpec(memory_space=pltpu.SMEM)
    n_classes = len(CLASSES)

    def buf(*shape, dtype=BF16):
        return pltpu.VMEM(shape, dtype)

    return pl.pallas_call(
        functools.partial(kernel, N_SEND),
        out_shape=(
            jax.ShapeDtypeStruct((1, 2, OWN_HEADS, LATENT), BF16),
            jax.ShapeDtypeStruct((ROWS, WIDTH), BF16),
        ),
        in_specs=[hbm, hbm, smem, hbm, vmem, vmem, hbm, hbm],
        out_specs=(vmem, vmem),
        scratch_shapes=[
            buf(2, 576, HEADS),
            buf(576, KEYS),
            buf(2, NX, WIDTH, UNITS),
            buf(NX, 256, WIDTH),
            buf(n_classes, SLOTS, WIDTH + TABLE),
            buf(n_classes, SLOTS, WIDTH),
            buf(n_classes, SLOTS, SLOTS),
            buf(2, n_classes * SLOTS, WIDTH),
            buf(2, 3, 2 * SLOTS, UNITS),
            buf(2, 3, 2 * SLOTS, UNITS),
            buf(2, 2 * SLOTS, UNITS, dtype=F32),
            buf(2, 2 * SLOTS, UNITS),
            buf(2, 2 * SLOTS, UNITS),
            buf(n_classes, SLOTS, WIDTH),
            buf(n_classes, SLOTS, WIDTH),
            buf(2, 2 * SLOTS, WIDTH, dtype=F32),
            buf(2, 2, 2 * SLOTS, WIDTH, dtype=F32),
            buf(n_classes, 2, SLOTS, WIDTH),
            buf(n_classes, 2, SLOTS, WIDTH),
            buf(n_classes, SLOTS, WIDTH),
            buf(n_classes, SLOTS, WIDTH),
            buf(3, SLOTS, WIDTH),
            buf(2, SLOTS, WIDTH),
            buf(2 * ROWS, WIDTH),
            buf(2 * ROWS, WIDTH),
            buf(SLOTS, WIDTH, dtype=F32),
            buf(3, ROWS, WIDTH),
            buf(3, ROWS, WIDTH),
            buf(2, HEADS, LATENT),
            buf(2, HEADS, 128, dtype=F32),
            buf(7, 2, OWN_HEADS, LATENT),
            buf(7, 2, OWN_HEADS, 128, dtype=F32),
            pltpu.SemaphoreType.DMA((9,)),
            pltpu.SemaphoreType.DMA((N_SEND,)),
            pltpu.SemaphoreType.DMA((N_SEND,)),
        ],
        compiler_params=pltpu.CompilerParams(
            collective_id=0, has_side_effects=True, vmem_limit_bytes=VMEM_LIMIT
        ),
    )(queries, cache, lengths, tokens, ids.T, gates.T, up, down)


def solution(mesh):
    in_specs = (
        P("exp", None, None, None),
        P("exp", None, "ctx"),
        P("exp"),
        P("exp", None),
        P("exp", None),
        P("exp", None),
        P("exp", None, "ctx"),
        P("exp", "ctx", None),
    )
    out_specs = (P("exp", None, "ctx", None), P("exp", "ctx"))
    return jax.shard_map(shards, mesh=mesh, in_specs=in_specs, out_specs=out_specs, check_vma=False)
```
